256 devices in a mesh: row: 16 (over z, x_hi), col: 16 (over x_lo, y, core).
Axes of the slice: x: 4 (x_hi: 2, x_lo: 2; x = x_hi * 2 + x_lo), y: 4, z: 8, core: 2. Of those that a mesh axis runs over, the one named last changes fastest.
Arguments:
- inputs: bfloat16 [2048, 8192], P('row', 'col'), may hold values from -6 to 6
- cotangent: bfloat16 [2048, 32768], P('col', 'row'), may hold values from -6 to 6
- sparse_blocks: bfloat16 [16, 16, 16, 4096], P('col', 'row'), may hold values from -0.25 to 0.25
- block_index: int32 [16, 16, 16], P('col', 'row'), may hold values from 0 to 255, as said below
- u_factor: bfloat16 [8192, 256], P('col'), may hold values from -0.0625 to 0.0625
- v_factor: bfloat16 [256, 32768], P(None, 'row'), may hold values from -0.375 to 0.375
Outputs:
- hidden: bfloat16 [2048, 32768], P('col', 'row')
- input_grad: bfloat16 [2048, 8192], P('row', 'col')
- blocks_grad: bfloat16 [16, 16, 16, 4096], P('col', 'row')
- u_grad: float32 [8192, 256], P('col', 'row')
- v_grad: float32 [256, 32768], P('col', 'row')
The draws below stay inside these ranges and needn't reach their ends.
Inputs may be any that keep to these rules, and one draw needn't show every extreme that they name: `block_index`: within one shard (c, r) the 16 positions are distinct, each in 0 to 255.
All inputs are finite; a program needn't handle non-finite values.
Results may differ from the reference program's by a relative error of at most 0.015.
Values may be sent and summed in bfloat16 or wider, within the bound.
No kernel may reach another device: no remote copies, remote signals or barrier semaphores. Data moves between devices by JAX's collectives and lax.ppermute only.
A program may use at most 128 MiB of HBM per device.

```python
import jax
import jax.numpy as jnp
from jax import lax

D = 8192
FF = 32768
RANK = 256
BS = 64
LEVELS = 8
TOKENS = 2048
NB_SHARD = 16
N_ROW = 16
N_COL = 16


def draw_block_index(key, part):
    key = jax.random.fold_in(key, 7)
    cells = D // (N_COL * BS) * (FF // (N_ROW * BS))
    keys = jax.random.split(key, N_COL * N_ROW)
    picks = jax.vmap(lambda k: jax.random.permutation(k, cells)[:NB_SHARD])(keys)
    return picks.reshape(N_COL, N_ROW, NB_SHARD).astype(jnp.int32)


def block_levels(rng, dims, cuts, smallest, top_value):
    level = 1.0
    for position, shards_of in cuts:
        heights = jax.random.uniform(jax.random.fold_in(jax.random.fold_in(rng, 6), position), (shards_of,), jnp.float32, smallest / len(cuts), top_value / len(cuts))
        level = level * jnp.repeat(jnp.exp(heights), dims[position] // shards_of).reshape((-1,) + (1,) * (len(dims) - 1 - position))
    return level


def noise(stream_key, dims, deviation, limit, pieces=(), kind=jnp.bfloat16):
    result = jax.random.normal(stream_key, dims, jnp.float32) * deviation
    if len(pieces) > 0:
        result = block_levels(stream_key, dims, pieces, -0.22, 0.18) * result
    return jnp.clip(result, min=-limit, max=limit).astype(kind)


def setup_inputs(seed: int = 0) -> dict:
    seeds = jax.random.split(jax.random.key(seed), 7)
    inputs = noise(seeds[0], (TOKENS, D), 1.0, 6.0, ((0, 16), (1, 16)))
    cotangent = noise(seeds[1], (TOKENS, FF), 1.0, 6.0, ((0, 16), (1, 16)))
    sparse_blocks = noise(seeds[2], (N_COL, N_ROW, NB_SHARD, BS * BS), (LEVELS * BS) ** -0.5, 0.25, ((0, 16), (1, 16)))
    block_index = draw_block_index(jax.random.fold_in(seeds[6], 71), 0)
    u_factor = noise(seeds[4], (D, RANK), D ** -0.5, 0.0625, ((0, 16),))
    v_factor = noise(seeds[5], (RANK, FF), RANK ** -0.5, 0.375, ((1, 16),))
    return dict(inputs=inputs, cotangent=cotangent, sparse_blocks=sparse_blocks, block_index=block_index, u_factor=u_factor, v_factor=v_factor)


def gelu_value(z):
    return 0.5 * z * (1.0 + lax.erf(z * 0.7071067811865476))


def gelu_slope(z):
    return 0.5 * (1.0 + lax.erf(z * 0.7071067811865476)) + z * jnp.exp(-0.5 * z * z) * 0.3989422804014327


def select_tables(index, brows, bcols):
    rows_of = index // bcols
    cols_of = index % bcols
    onehot_rows = (rows_of[:, None] == jnp.arange(brows, dtype=jnp.int32)[None, :]).astype(jnp.float32)
    onehot_cols = (cols_of[:, None] == jnp.arange(bcols, dtype=jnp.int32)[None, :]).astype(jnp.float32)
    return onehot_rows, onehot_cols


def shard_forward(x_slice, blocks, index, bcols):
    count = x_slice.shape[0]
    brows = x_slice.shape[1] // BS
    onehot_rows, onehot_cols = select_tables(index, brows, bcols)
    xr = x_slice.astype(jnp.float32).reshape(count, brows, BS)
    picked = jnp.einsum('tkf,bk->tbf', xr, onehot_rows)
    weights = blocks.astype(jnp.float32).reshape(-1, BS, BS)
    products = jnp.einsum('tbf,bfg->tbg', picked, weights)
    return jnp.einsum('tbg,bc->tcg', products, onehot_cols).reshape(count, bcols * BS)


def shard_backward(x_slice, dz_slice, blocks, index, bcols):
    count = x_slice.shape[0]
    brows = x_slice.shape[1] // BS
    onehot_rows, onehot_cols = select_tables(index, brows, bcols)
    xr = x_slice.astype(jnp.float32).reshape(count, brows, BS)
    picked = jnp.einsum('tkf,bk->tbf', xr, onehot_rows)
    dzr = dz_slice.astype(jnp.float32).reshape(count, bcols, BS)
    dz_picked = jnp.einsum('tcg,bc->tbg', dzr, onehot_cols)
    weights = blocks.astype(jnp.float32).reshape(-1, BS, BS)
    block_grads = jnp.einsum('tbf,tbg->bfg', picked, dz_picked).reshape(-1, BS * BS)
    back = jnp.einsum('tbg,bfg->tbf', dz_picked, weights)
    x_part = jnp.einsum('tbf,bk->tkf', back, onehot_rows).reshape(count, brows * BS)
    return x_part, block_grads


def reference(inputs, cotangent, sparse_blocks, block_index, u_factor, v_factor):
    count = inputs.shape[0]
    width_c = D // N_COL
    width_r = FF // N_ROW
    bcols = width_r // BS
    slices = jnp.arange(N_COL, dtype=jnp.int32)
    hidden_slices = jnp.arange(N_ROW, dtype=jnp.int32)

    def col_step(total, c):
        x_slice = lax.dynamic_slice_in_dim(inputs, c * width_c, width_c, 1)
        parts = jax.vmap(lambda b, i: shard_forward(x_slice, b, i, bcols))(sparse_blocks[c], block_index[c])
        part = jnp.transpose(parts, (1, 0, 2)).reshape(count, FF).astype(jnp.bfloat16)
        part = lax.optimization_barrier(part)
        return total + part.astype(jnp.float32), None

    z_sparse, _ = lax.scan(col_step, jnp.zeros((count, FF), jnp.float32), slices)
    p_low = jnp.dot(inputs, u_factor, preferred_element_type=jnp.float32).astype(jnp.bfloat16)
    z_full = z_sparse + jnp.dot(p_low, v_factor, preferred_element_type=jnp.float32)
    hidden = gelu_value(z_full).astype(jnp.bfloat16)
    dz_full = (cotangent.astype(jnp.float32) * gelu_slope(z_full)).astype(jnp.bfloat16)
    q_full = jnp.dot(dz_full, v_factor.T, preferred_element_type=jnp.float32)

    def back_step(carry, c):
        x_slice = lax.dynamic_slice_in_dim(inputs, c * width_c, width_c, 1)

        def one(blocks, index, r):
            dz_slice = lax.dynamic_slice_in_dim(dz_full, r * width_r, width_r, 1)
            return shard_backward(x_slice, dz_slice, blocks, index, bcols)

        x_parts, grads = jax.vmap(one)(sparse_blocks[c], block_index[c], hidden_slices)
        return carry, (jnp.sum(x_parts, axis=0), grads)

    _, (x_parts, grads) = lax.scan(back_step, jnp.zeros((), jnp.float32), slices)
    dx_sparse = jnp.transpose(x_parts, (1, 0, 2)).reshape(count, D)
    dx_low = jnp.dot(q_full, u_factor.astype(jnp.float32).T, precision=lax.Precision.HIGHEST)
    input_grad = (dx_sparse + dx_low).astype(jnp.bfloat16)
    blocks_grad = grads.astype(jnp.bfloat16)
    u_grad = jnp.dot(inputs.astype(jnp.float32).T, q_full, precision=lax.Precision.HIGHEST)
    v_grad = jnp.dot(p_low.T, dz_full, preferred_element_type=jnp.float32)
    return hidden, input_grad, blocks_grad, u_grad, v_grad
```

```python
import functools

import jax
import jax.numpy as jnp
from jax import lax
from jax.experimental import pallas as pl
from jax.experimental.pallas import tpu as pltpu
from jax.sharding import Mesh, PartitionSpec as P

BS = 64
NB = 16
SH = 16
NZ = 8
NK = 8
FEAT = 512
WIDTH = 2048
TOK = 128
RANK = 256
RS = RANK // SH
WROWS = FEAT + 16
VROWS = WIDTH // TOK * RS
UROWS = FEAT // TOK * RS
BCOLS = WIDTH // BS

ROW = ("z", "xh")
COL = ("xl", "y", "core")
ALL = ROW + COL

NN = (((1,), (0,)), ((), ()))
NT = (((1,), (1,)), ((), ()))
F32 = jnp.float32
BF16 = jnp.bfloat16


def dot(a, b, dims):
    return lax.dot_general(a, b, dims, preferred_element_type=F32)


def gelu_pair(z):
    half = 0.5 * (1.0 + lax.erf(z * 0.7071067811865476))
    slope = half + z * jnp.exp(-0.5 * z * z) * 0.3989422804014327
    return z * half, slope


def block_start(position):
    return pl.multiple_of(position * BS, BS)


def x_slot(place, s):
    return (((s >> 1) - place[0]) & (NZ - 1)) * 2 + ((s & 1) ^ place[1])


def x_shard(place, slot):
    return (((slot >> 1) + place[0]) & (NZ - 1)) * 2 + ((slot & 1) ^ place[1])


def w_slot(place, s):
    return ((s & 1) ^ place[2]) * NK + (s >> 1)


def forward_kernel(place, index, *refs):
    x_parts = refs[: 2 * NZ]
    w_own, w_other, p_t, v, cot, hidden, dz_t, q_t, x, w, z_t, sems = refs[2 * NZ :]
    copies = [
        pltpu.make_async_copy(w_own, w.at[:NK], sems.at[2 * NZ]),
        pltpu.make_async_copy(w_other, w.at[NK:], sems.at[2 * NZ + 1]),
    ]
    for slot in range(2 * NZ):
        copies.append(pltpu.make_async_copy(x_parts[slot], x.at[slot], sems.at[slot]))
    for copy in copies:
        copy.start()
    z_t[...] = jnp.zeros_like(z_t)
    for copy in copies:
        copy.wait()

    def shard(slot, carry):
        s = w_slot(place, x_shard(place, slot))
        sums = []
        for pair in range(NB // 2):
            both = w[s, pair * BS : (pair + 1) * BS, :].T
            for side in range(2):
                b = index[s, 2 * pair + side]
                x_block = x[slot, pl.ds(block_start(b // BCOLS), BS), :]
                sums.append((b % BCOLS, dot(both[side * BS : (side + 1) * BS], x_block, NN)))
        for where, value in sums:
            z_t[pl.ds(block_start(where), BS), :] += value
        return carry

    lax.fori_loop(0, SH, shard, 0)
    p = p_t[...].T
    for j in range(WIDTH // TOK):
        part = slice(j * TOK, (j + 1) * TOK)
        z = z_t[part, :].T + dot(p, v[:, part], NN)
        value, slope = gelu_pair(z)
        hidden[:, part] = value.astype(BF16)
        dz = cot[:, part].astype(F32) * slope
        dz_t[part, :] = dz.T.astype(BF16)
    q_t[...] = dot(v[...], dz_t[...], NN)


def back_kernel(slots, place, index, w, dz_t, *refs):
    outs = refs[: len(slots)]
    total, done = refs[len(slots) :]

    def shard(i, carry):
        slot = (i + slots[0]) & (2 * NZ - 1)
        s = w_slot(place, x_shard(place, slot))
        total[...] = jnp.zeros_like(total)
        sums = []
        for pair in range(NB // 2):
            both = w[s, pair * BS : (pair + 1) * BS, :]
            for side in range(2):
                b = index[s, 2 * pair + side]
                dz_block = dz_t[pl.ds(block_start(b % BCOLS), BS), :]
                sums.append((b // BCOLS, dot(both[:, side * BS : (side + 1) * BS], dz_block, NN)))
        for where, value in sums:
            total[pl.ds(block_start(where), BS), :] += value
        done[i] = total[...].astype(BF16)
        return carry

    lax.fori_loop(0, len(slots), shard, 0)
    for i in range(len(slots)):
        outs[i][...] = done[i]


def grad_rows(place, index, x, dz_t, p_t, out, half, other):
    core = place[2] ^ half

    def plus(value, k, first):
        if other is not None:
            value += other[k, first : first + value.shape[0], :].astype(F32)
        return value.astype(BF16)

    def shard(k, carry):
        slot = x_slot(place, 2 * k + core)
        for pair in range(NB // 2):
            halves = []
            for side in range(2):
                b = index[half * NK + k, 2 * pair + side]
                x_block = x[slot, pl.ds(block_start(b // BCOLS), BS), :]
                dz_block = dz_t[pl.ds(block_start(b % BCOLS), BS), :]
                halves.append(dot(x_block, dz_block, NT))
            both = jnp.concatenate(halves, axis=1)
            out[k, pair * BS : (pair + 1) * BS, :] = plus(both, k, pair * BS)
        return carry

    lax.fori_loop(0, NK, shard, 0)
    p = jnp.concatenate([p_t[2 * k + core] for k in range(NK)], axis=0)
    for j in range(WIDTH // TOK):
        part = dot(p, dz_t[j * TOK : (j + 1) * TOK, :], NT)
        first = FEAT + j * RS
        for k in range(NK):
            out[k, first : first + RS, :] = plus(part[k * RS : (k + 1) * RS], k, first)


def grad_other_kernel(place, index, x, dz_t, p_t, out):
    grad_rows(place, index, x, dz_t, p_t, out, 1, None)


def grad_own_kernel(place, index, x, dz_t, p_t, q_t, other, out):
    grad_rows(place, index, x, dz_t, p_t, out, 0, other)
    q = q_t[place[3]]

    def shard(k, carry):
        for half in range(2):
            u = dot(q, x[x_slot(place, 2 * k + (place[2] ^ half))], NT).astype(BF16)
            for j in range(FEAT // TOK):
                first = FEAT + VROWS + half * UROWS + j * RS
                out[k, first : first + RS, :] = u[:, j * TOK : (j + 1) * TOK]
        return carry

    lax.fori_loop(0, NK, shard, 0)


def call(kernel, out_shape, flops, bytes_accessed, operands, scratch=(), free=0):
    vmem = pl.BlockSpec(memory_space=pltpu.VMEM)
    smem = pl.BlockSpec(memory_space=pltpu.SMEM)
    anywhere = pl.BlockSpec(memory_space=pltpu.HBM)
    many = isinstance(out_shape, tuple)
    return pl.pallas_call(
        kernel,
        out_shape=out_shape,
        in_specs=[smem] * 2 + [anywhere] * free + [vmem] * (len(operands) - 2 - free),
        out_specs=(vmem,) * len(out_shape) if many else vmem,
        scratch_shapes=list(scratch),
        compiler_params=pltpu.CompilerParams(vmem_limit_bytes=16 << 20),
        cost_estimate=pl.CostEstimate(
            flops=flops, bytes_accessed=bytes_accessed, transcendentals=0
        ),
    )(*operands)


def shape(*dims, kind=BF16):
    return jax.ShapeDtypeStruct(dims, kind)


def add(*terms):
    return sum(t.astype(F32) for t in terms).astype(BF16)


def shift(x, by):
    return lax.ppermute(x, "z", [(i, (i + by) % NZ) for i in range(NZ)])


def gather_ring(own):
    held = {0: own}
    for step in range(1, NZ // 2):
        held[-step] = shift(held[1 - step], 1)
        held[step] = shift(held[step - 1], -1)
    return held


def meet(x, axis, flip):
    count = {"z": 8, "xh": 2, "xl": 2, "y": 4, "core": 2}[axis]
    return lax.ppermute(x, axis, [(i, i ^ flip) for i in range(count)])


def on_device(inputs, cotangent, sparse_blocks, block_index, u_factor, v_factor):
    turn = [(r * SH + c, c * SH + r) for r in range(SH) for c in range(SH)]
    place = jnp.stack(
        [lax.axis_index("z"), lax.axis_index("xh"), lax.axis_index("core"), lax.axis_index(ROW)]
    ).astype(jnp.int32)

    w_pairs = sparse_blocks.reshape(NB // 2, 2, BS, BS).transpose(0, 2, 1, 3).reshape(FEAT, 2 * BS)
    index_row = jnp.zeros((16, TOK), BF16).at[0, :NB].set(block_index.reshape(NB).astype(BF16))
    w_mine, mine = lax.optimization_barrier((jnp.concatenate([w_pairs, index_row]), inputs.T))
    w_own = lax.all_gather(w_mine, ("xl", "y"), axis=0)

    turned = lax.ppermute(mine, ALL, turn)
    p = lax.dot_general(u_factor, mine, (((0,), (0,)), ((), ())), preferred_element_type=F32)
    p = p + meet(p, "core", 1)
    turned, p = lax.optimization_barrier((turned, p))
    rings = [gather_ring(turned), gather_ring(meet(turned, "xh", 1))]
    rings[0][4] = shift(rings[0][-3], 1)
    rings[1][4] = shift(rings[1][3], -1)
    x_parts = [rings[j][rel if rel <= 4 else rel - NZ] for rel in range(NZ) for j in range(2)]
    for axis, flip in (("xl", 1), ("y", 1), ("y", 2)):
        p = p + meet(p, axis, flip)
    thirds = [ring[i] for ring in rings for i in (3, -3)]
    w_own, p, _ = lax.optimization_barrier((w_own, p.astype(BF16), thirds))
    w_other = meet(w_own, "core", 1)
    p_t = lax.ppermute(p, ALL, turn)
    index = jnp.concatenate([w_own[:, FEAT, :NB], w_other[:, FEAT, :NB]]).astype(jnp.int32)

    hidden, dz_t, q, x_all, w_all = call(
        forward_kernel,
        (
            shape(TOK, WIDTH),
            shape(WIDTH, TOK),
            shape(RANK, TOK, kind=F32),
            shape(SH, FEAT, TOK),
            shape(SH, WROWS, TOK),
        ),
        800_000_000,
        10 << 20,
        (place, index, *x_parts, w_own, w_other, p_t, v_factor, cotangent),
        [pltpu.VMEM((WIDTH, TOK), F32), pltpu.SemaphoreType.DMA((2 * NZ + 2,))],
        free=2 * NZ + 2,
    )
    back = {}
    for slots in (range(6, 12), range(12, 22)):
        parts = call(
            functools.partial(back_kernel, slots),
            (shape(FEAT, TOK),) * len(slots),
            20_000_000 * len(slots),
            len(slots) << 19,
            (place, index, w_all, dz_t),
            [pltpu.VMEM((FEAT, TOK), F32), pltpu.VMEM((len(slots), FEAT, TOK), BF16)],
        )
        back.update({slot % (2 * NZ): part for slot, part in zip(slots, parts)})

    def own(rel, j):
        return back[2 * (rel % NZ) + j]

    q, _ = lax.optimization_barrier((q, back[0]))
    for axis, flip in (("z", 1), ("z", 2), ("z", 4), ("xh", 1)):
        q = q + meet(q.astype(BF16), axis, flip).astype(F32)
    q_t = q.astype(BF16)

    p_slices = p_t.reshape(SH, RS, TOK)
    grads = call(
        grad_other_kernel,
        shape(NK, FEAT + VROWS, TOK),
        200_000_000,
        4 << 20,
        (place, index, x_all, dz_t, p_slices),
    )
    grads = call(
        grad_own_kernel,
        shape(NK, FEAT + VROWS + 2 * UROWS, TOK),
        300_000_000,
        6 << 20,
        (place, index, x_all, dz_t, p_slices, q_t.reshape(SH, RS, TOK), meet(grads, "core", 1)),
    )
    up = [own(3, 0), own(3, 1)]
    down = [own(-3, 0), own(-3, 1)]
    up[0] = add(up[0], shift(own(4, 0), 1))
    down[1] = add(down[1], shift(own(4, 1), -1))
    for rel in (2, 1):
        if rel == 1:
            grads, up[0] = lax.optimization_barrier((grads, up[0]))
        for j in range(2):
            up[j] = add(own(rel, j), shift(up[j], 1))
            down[j] = add(own(-rel, j), shift(down[j], -1))
    other = add(own(0, 1), shift(up[1], 1), shift(down[1], -1))
    total = add(own(0, 0), shift(up[0], 1), shift(down[0], -1), meet(other, "xh", 1))
    x_grad_t = lax.ppermute(total, ALL, turn)
    grads_in = lax.all_to_all(grads, ("xl", "y"), 0, 0)

    q_turned = lax.ppermute(q_t, ALL, turn)
    x_low = lax.dot_general(
        q_turned, u_factor, (((0,), (1,)), ((), ())), preferred_element_type=F32
    )
    input_grad = add(x_grad_t.T, x_low)

    grads_sum = jnp.sum(grads_in.astype(F32), axis=0)
    blocks_grad = (
        grads_sum[:FEAT]
        .astype(BF16)
        .reshape(NB // 2, BS, 2, BS)
        .transpose(0, 2, 1, 3)
        .reshape(sparse_blocks.shape)
    )
    v_grad = (
        grads_sum[FEAT : FEAT + VROWS]
        .reshape(WIDTH // TOK, RS, TOK)
        .transpose(1, 0, 2)
        .reshape(RS, WIDTH)
    )
    u_own = grads_sum[FEAT + VROWS : FEAT + VROWS + UROWS]
    u_other = grads_sum[FEAT + VROWS + UROWS :]
    u_grad = (
        (u_own + meet(u_other, "core", 1))
        .reshape(FEAT // TOK, RS, TOK)
        .transpose(0, 2, 1)
        .reshape(FEAT, RS)
    )
    return hidden, input_grad, blocks_grad, u_grad, v_grad


def solution(mesh):
    fine = Mesh(mesh.devices.reshape(8, 2, 2, 4, 2), ALL)
    in_specs = (
        P(ROW, COL),
        P(COL, ROW),
        P(COL, ROW, None, None),
        P(COL, ROW, None),
        P(COL, None),
        P(None, ROW),
    )
    out_specs = (
        P(COL, ROW),
        P(ROW, COL),
        P(COL, ROW, None, None),
        P(COL, ROW),
        P(COL, ROW),
    )
    return jax.shard_map(
        on_device, mesh=fine, in_specs=in_specs, out_specs=out_specs, check_vma=False
    )
```

```python
import functools

import jax
import jax.numpy as jnp
from jax import lax
from jax.experimental import pallas as pl
from jax.experimental.pallas import tpu as pltpu
from jax.sharding import Mesh, PartitionSpec as P

BS = 64
NB = 16
SH = 16
NZ = 8
NK = 8
FEAT = 512
WIDTH = 2048
TOK = 128
RANK = 256
RS = RANK // SH
ROWS = FEAT + RS
WROWS = FEAT + 16
VROWS = WIDTH // TOK * RS
UROWS = FEAT // TOK * RS
BCOLS = WIDTH // BS

ROW = ("z", "xh")
COL = ("xl", "y", "core")
ALL = ROW + COL

NN = (((1,), (0,)), ((), ()))
NT = (((1,), (1,)), ((), ()))
F32 = jnp.float32
BF16 = jnp.bfloat16


def dot(a, b, dims):
    return lax.dot_general(a, b, dims, preferred_element_type=F32)


def gelu_pair(z):
    half = 0.5 * (1.0 + lax.erf(z * 0.7071067811865476))
    slope = half + z * jnp.exp(-0.5 * z * z) * 0.3989422804014327
    return z * half, slope


def block_start(position):
    return pl.multiple_of(position * BS, BS)


def x_slot(place, s):
    return (((s >> 1) - place[0]) & (NZ - 1)) * 2 + ((s & 1) ^ place[1])


def x_shard(place, slot):
    return (((slot >> 1) + place[0]) & (NZ - 1)) * 2 + ((slot & 1) ^ place[1])


def first_kernel(x, u, x_t, p):
    x_t[...] = x[...].T
    p[...] = dot(u[...].T, x_t[...], NN).reshape(SH, RS, TOK)


def forward_kernel(place, index, *refs):
    x_parts = refs[:NZ]
    w, v, cot, hidden, dz_t, q_t, x, z_t, sems = refs[NZ:]
    copies = [
        pltpu.make_async_copy(x_parts[rel], x.at[2 * rel : 2 * rel + 2], sems.at[rel])
        for rel in range(NZ)
    ]
    for copy in copies:
        copy.start()
    z_t[...] = jnp.zeros_like(z_t)
    for copy in copies:
        copy.wait()

    def shard(slot, carry):
        s = x_shard(place, slot)
        sums = []
        for pair in range(NB // 2):
            both = w[s, pair * BS : (pair + 1) * BS, :].T
            for side in range(2):
                b = index[s, 2 * pair + side]
                x_block = x[slot, pl.ds(block_start(b // BCOLS), BS), :]
                sums.append((b % BCOLS, dot(both[side * BS : (side + 1) * BS], x_block, NN)))
        for where, value in sums:
            z_t[pl.ds(block_start(where), BS), :] += value
        return carry

    lax.fori_loop(0, SH, shard, 0)
    p = jnp.concatenate([x[x_slot(place, s), FEAT:, :] for s in range(SH)], axis=0).T
    for j in range(WIDTH // TOK):
        part = slice(j * TOK, (j + 1) * TOK)
        z = z_t[part, :].T + dot(p, v[:, part], NN)
        value, slope = gelu_pair(z)
        hidden[:, part] = value.astype(BF16)
        dz = cot[:, part].astype(F32) * slope
        dz_t[part, :] = dz.T.astype(BF16)
    q_t[...] = dot(v[...], dz_t[...], NN)


def back_kernel(slots, place, index, w, dz_t, *refs):
    outs = refs[: len(slots) // 2]
    total, done = refs[len(slots) // 2 :]

    def shard(i, carry):
        slot = (i + slots[0]) & (2 * NZ - 1)
        s = x_shard(place, slot)
        total[...] = jnp.zeros_like(total)
        sums = []
        for pair in range(NB // 2):
            both = w[s, pair * BS : (pair + 1) * BS, :]
            for side in range(2):
                b = index[s, 2 * pair + side]
                dz_block = dz_t[pl.ds(block_start(b % BCOLS), BS), :]
                sums.append((b // BCOLS, dot(both[:, side * BS : (side + 1) * BS], dz_block, NN)))
        for where, value in sums:
            total[pl.ds(block_start(where), BS), :] += value
        done[i] = total[...].astype(BF16)
        return carry

    lax.fori_loop(0, len(slots), shard, 0)
    for i in range(len(slots) // 2):
        outs[i][...] = done[2 * i : 2 * i + 2]


def grad_rows(place, index, x, dz_t, out, half, other):
    core = place[2] ^ half

    def plus(value, k, first):
        if other is not None:
            value += other[k, first : first + value.shape[0], :].astype(F32)
        return value.astype(BF16)

    def shard(k, carry):
        s = 2 * k + core
        slot = x_slot(place, s)
        for pair in range(NB // 2):
            halves = []
            for side in range(2):
                b = index[s, 2 * pair + side]
                x_block = x[slot, pl.ds(block_start(b // BCOLS), BS), :]
                dz_block = dz_t[pl.ds(block_start(b % BCOLS), BS), :]
                halves.append(dot(x_block, dz_block, NT))
            both = jnp.concatenate(halves, axis=1)
            out[k, pair * BS : (pair + 1) * BS, :] = plus(both, k, pair * BS)
        return carry

    lax.fori_loop(0, NK, shard, 0)
    p = jnp.concatenate([x[x_slot(place, 2 * k + core), FEAT:, :] for k in range(NK)], axis=0)
    for j in range(WIDTH // TOK):
        part = dot(p, dz_t[j * TOK : (j + 1) * TOK, :], NT)
        first = FEAT + j * RS
        for k in range(NK):
            out[k, first : first + RS, :] = plus(part[k * RS : (k + 1) * RS], k, first)


def grad_other_kernel(place, index, x, dz_t, out):
    grad_rows(place, index, x, dz_t, out, 1, None)


def grad_own_kernel(place, index, x, dz_t, q_t, other, out):
    grad_rows(place, index, x, dz_t, out, 0, other)
    q = q_t[place[3]]

    def shard(k, carry):
        for half in range(2):
            slot = x_slot(place, 2 * k + (place[2] ^ half))
            u = dot(q, x[slot, :FEAT, :], NT).astype(BF16)
            for j in range(FEAT // TOK):
                first = FEAT + VROWS + half * UROWS + j * RS
                out[k, first : first + RS, :] = u[:, j * TOK : (j + 1) * TOK]
        return carry

    lax.fori_loop(0, NK, shard, 0)


def call(kernel, out_shape, flops, bytes_accessed, operands, scratch=(), free=0, scalars=2):
    vmem = pl.BlockSpec(memory_space=pltpu.VMEM)
    smem = pl.BlockSpec(memory_space=pltpu.SMEM)
    anywhere = pl.BlockSpec(memory_space=pl.ANY)
    many = isinstance(out_shape, tuple)
    return pl.pallas_call(
        kernel,
        out_shape=out_shape,
        in_specs=[smem] * scalars + [anywhere] * free + [vmem] * (len(operands) - scalars - free),
        out_specs=(vmem,) * len(out_shape) if many else vmem,
        scratch_shapes=list(scratch),
        compiler_params=pltpu.CompilerParams(vmem_limit_bytes=10 << 20),
        cost_estimate=pl.CostEstimate(
            flops=flops, bytes_accessed=bytes_accessed, transcendentals=0
        ),
    )(*operands)


def shape(*dims, kind=BF16):
    return jax.ShapeDtypeStruct(dims, kind)


def add(*terms):
    return sum(t.astype(F32) for t in terms).astype(BF16)


def shift(x, by):
    return lax.ppermute(x, "z", [(i, (i + by) % NZ) for i in range(NZ)])


def gather_ring(own):
    held = {0: own, -1: shift(own, 1), 1: shift(own, -1)}
    for step in (1, 2):
        held[-step - 1] = shift(held[-step], 1)
        held[step + 1] = shift(held[step], -1)
    held[4] = shift(held[-3], 1)
    return [held[rel if rel <= 4 else rel - NZ] for rel in range(NZ)]


def meet(x, axis, flip):
    count = {"z": 8, "xh": 2, "xl": 2, "y": 4, "core": 2}[axis]
    return lax.ppermute(x, axis, [(i, i ^ flip) for i in range(count)])


def on_device(inputs, cotangent, sparse_blocks, block_index, u_factor, v_factor):
    turn = [(r * SH + c, c * SH + r) for r in range(SH) for c in range(SH)]
    turn_pair = [(r * SH + c, (c ^ 1) * SH + r) for r in range(SH) for c in range(SH)]
    place = jnp.stack(
        [lax.axis_index("z"), lax.axis_index("xh"), lax.axis_index("core"), lax.axis_index(ROW)]
    ).astype(jnp.int32)

    w_pairs = sparse_blocks.reshape(NB // 2, 2, BS, BS).transpose(0, 2, 1, 3).reshape(FEAT, 2 * BS)
    index_row = jnp.zeros((16, TOK), BF16).at[0, :NB].set(block_index.reshape(NB).astype(BF16))
    w_mine = jnp.concatenate([w_pairs, index_row])
    w_mine, inputs = lax.optimization_barrier((w_mine, inputs))
    w_all = lax.all_gather(w_mine, COL, axis=0)
    index = w_all[:, FEAT, :NB].astype(jnp.int32)

    mine, p = call(
        first_kernel,
        (shape(FEAT, TOK), shape(SH, RS, TOK, kind=F32)),
        40_000_000,
        1 << 19,
        (inputs, u_factor),
        scalars=0,
    )
    turned = lax.ppermute(mine, ALL, turn)
    p_in = lax.all_to_all(p, COL, 0, 0)
    turned, p_in = lax.optimization_barrier((turned, p_in))
    p = jnp.sum(p_in, axis=0).astype(BF16)
    parts = [
        turned,
        lax.ppermute(p, ALL, turn),
        meet(turned, "xh", 1),
        lax.ppermute(p, ALL, turn_pair),
    ]
    x_parts = gather_ring(jnp.concatenate(parts).reshape(2, ROWS, TOK))

    hidden, dz_t, q, x_all = call(
        forward_kernel,
        (
            shape(TOK, WIDTH),
            shape(WIDTH, TOK),
            shape(RANK, TOK, kind=F32),
            shape(SH, ROWS, TOK),
        ),
        800_000_000,
        10 << 20,
        (place, index, *x_parts, w_all, v_factor, cotangent),
        [pltpu.VMEM((WIDTH, TOK), F32), pltpu.SemaphoreType.DMA((NZ,))],
        free=NZ,
    )

    back = {}
    dz_back = dz_t
    for slots in (range(6, 12), range(12, 22)):
        outs = call(
            functools.partial(back_kernel, slots),
            (shape(2, FEAT, TOK),) * (len(slots) // 2),
            20_000_000 * len(slots),
            len(slots) << 19,
            (place, index, w_all, dz_back),
            [pltpu.VMEM((FEAT, TOK), F32), pltpu.VMEM((len(slots), FEAT, TOK), BF16)],
        )
        back.update({slot // 2 % NZ: part for slot, part in zip(slots[::2], outs)})
        dz_back, back[3] = lax.optimization_barrier((dz_back, back[3]))

    up, down = shift(back[4], 1), shift(back[5], -1)
    q, up, down, back[0] = lax.optimization_barrier((q, up, down, back[0]))
    up = add(back[3], up)
    for axis, flip in (("z", 1), ("z", 2), ("z", 4), ("xh", 1)):
        q = q + meet(q.astype(BF16), axis, flip).astype(F32)
    q_t = q.astype(BF16)

    grads = call(
        grad_other_kernel,
        shape(NK, FEAT + VROWS, TOK),
        200_000_000,
        4 << 20,
        (place, index, x_all, dz_t),
    )
    grads = call(
        grad_own_kernel,
        shape(NK, FEAT + VROWS + 2 * UROWS, TOK),
        300_000_000,
        6 << 20,
        (place, index, x_all, dz_t, q_t.reshape(SH, RS, TOK), meet(grads, "core", 1)),
    )

    down = add(back[6], down)
    up = add(back[2], shift(up, 1))
    down = add(back[7], shift(down, -1))
    up = add(back[1], shift(up, 1))
    up, down = shift(up, 1), shift(down, -1)
    grads, up, down = lax.optimization_barrier((grads, up, down))
    other = add(back[0][1], up[1], down[1])
    total = add(back[0][0], up[0], down[0], meet(other, "xh", 1))
    x_grad_t = lax.ppermute(total, ALL, turn)
    grads_in = lax.all_to_all(grads, ("xl", "y"), 0, 0)
    q_turned = lax.ppermute(q_t, ALL, turn)

    grads_sum = jnp.sum(grads_in.astype(F32), axis=0)
    blocks_grad = (
        grads_sum[:FEAT]
        .astype(BF16)
        .reshape(NB // 2, BS, 2, BS)
        .transpose(0, 2, 1, 3)
        .reshape(sparse_blocks.shape)
    )
    v_grad = (
        grads_sum[FEAT : FEAT + VROWS]
        .reshape(WIDTH // TOK, RS, TOK)
        .transpose(1, 0, 2)
        .reshape(RS, WIDTH)
    )
    u_own = grads_sum[FEAT + VROWS : FEAT + VROWS + UROWS]
    u_other = grads_sum[FEAT + VROWS + UROWS :]
    u_grad = (
        (u_own + meet(u_other, "core", 1))
        .reshape(FEAT // TOK, RS, TOK)
        .transpose(0, 2, 1)
        .reshape(FEAT, RS)
    )
    x_low = lax.dot_general(
        q_turned, u_factor, (((0,), (1,)), ((), ())), preferred_element_type=F32
    )
    x_grad_t, x_low, blocks_grad, v_grad, u_grad = lax.optimization_barrier(
        (x_grad_t, x_low, blocks_grad, v_grad, u_grad)
    )
    input_grad = add(x_grad_t.T, x_low)
    return hidden, input_grad, blocks_grad, u_grad, v_grad


def solution(mesh):
    fine = Mesh(mesh.devices.reshape(8, 2, 2, 4, 2), ALL)
    in_specs = (
        P(ROW, COL),
        P(COL, ROW),
        P(COL, ROW, None, None),
        P(COL, ROW, None),
        P(COL, None),
        P(None, ROW),
    )
    out_specs = (
        P(COL, ROW),
        P(ROW, COL),
        P(COL, ROW, None, None),
        P(COL, ROW),
        P(COL, ROW),
    )
    return jax.shard_map(
        on_device, mesh=fine, in_specs=in_specs, out_specs=out_specs, check_vma=False
    )
```

```python
import functools

import jax
import jax.numpy as jnp
from jax import lax
from jax.experimental import pallas as pl
from jax.experimental.pallas import tpu as pltpu
from jax.sharding import Mesh, PartitionSpec as P

BS = 64
NB = 16
SH = 16
NZ = 8
NK = 8
FEAT = 512
WIDTH = 2048
TOK = 128
RANK = 256
RS = RANK // SH
WROWS = FEAT + 16
VROWS = WIDTH // TOK * RS
UROWS = FEAT // TOK * RS
BCOLS = WIDTH // BS

ROW = ("z", "xh")
COL = ("xl", "y", "core")
ALL = ROW + COL

NN = (((1,), (0,)), ((), ()))
NT = (((1,), (1,)), ((), ()))
F32 = jnp.float32
BF16 = jnp.bfloat16


def dot(a, b, dims):
    return lax.dot_general(a, b, dims, preferred_element_type=F32)


def gelu_pair(z):
    half = 0.5 * (1.0 + lax.erf(z * 0.7071067811865476))
    slope = half + z * jnp.exp(-0.5 * z * z) * 0.3989422804014327
    return z * half, slope


def block_start(position):
    return pl.multiple_of(position * BS, BS)


def x_slot(place, s):
    return (((s >> 1) - place[0]) & (NZ - 1)) * 2 + ((s & 1) ^ place[1])


def x_shard(place, slot):
    return (((slot >> 1) + place[0]) & (NZ - 1)) * 2 + ((slot & 1) ^ place[1])


def first_kernel(x, u, x_t, p):
    x_t[...] = x[...].T
    p[...] = dot(u[...].T, x_t[...], NN)


def forward_kernel(place, index, *refs):
    x_parts = refs[:NZ]
    w, p_t, v, cot, hidden, dz_t, q_t, x, z_t, sems = refs[NZ:]
    copies = [
        pltpu.make_async_copy(x_parts[rel], x.at[2 * rel : 2 * rel + 2], sems.at[rel])
        for rel in range(NZ)
    ]
    for copy in copies:
        copy.start()
    z_t[...] = jnp.zeros_like(z_t)
    for copy in copies:
        copy.wait()

    def shard(slot, carry):
        s = x_shard(place, slot)
        sums = []
        for pair in range(NB // 2):
            both = w[s, pair * BS : (pair + 1) * BS, :].T
            for side in range(2):
                b = index[s, 2 * pair + side]
                x_block = x[slot, pl.ds(block_start(b // BCOLS), BS), :]
                sums.append((b % BCOLS, dot(both[side * BS : (side + 1) * BS], x_block, NN)))
        for where, value in sums:
            z_t[pl.ds(block_start(where), BS), :] += value
        return carry

    lax.fori_loop(0, SH, shard, 0)
    p = p_t[...].T
    for j in range(WIDTH // TOK):
        part = slice(j * TOK, (j + 1) * TOK)
        z = z_t[part, :].T + dot(p, v[:, part], NN)
        value, slope = gelu_pair(z)
        hidden[:, part] = value.astype(BF16)
        dz = cot[:, part].astype(F32) * slope
        dz_t[part, :] = dz.T.astype(BF16)
    q_t[...] = dot(v[...], dz_t[...], NN)


def back_kernel(slots, place, index, w, dz_t, *refs):
    outs = refs[: len(slots) // 2]
    total, done = refs[len(slots) // 2 :]

    def shard(i, carry):
        slot = (i + slots[0]) & (2 * NZ - 1)
        s = x_shard(place, slot)
        total[...] = jnp.zeros_like(total)
        sums = []
        for pair in range(NB // 2):
            both = w[s, pair * BS : (pair + 1) * BS, :]
            for side in range(2):
                b = index[s, 2 * pair + side]
                dz_block = dz_t[pl.ds(block_start(b % BCOLS), BS), :]
                sums.append((b // BCOLS, dot(both[:, side * BS : (side + 1) * BS], dz_block, NN)))
        for where, value in sums:
            total[pl.ds(block_start(where), BS), :] += value
        done[i] = total[...].astype(BF16)
        return carry

    lax.fori_loop(0, len(slots), shard, 0)
    for i in range(len(slots) // 2):
        outs[i][...] = done[2 * i : 2 * i + 2]


def grad_rows(place, index, x, dz_t, p_t, out, half, other):
    core = place[2] ^ half

    def plus(value, k, first):
        if other is not None:
            value += other[k, first : first + value.shape[0], :].astype(F32)
        return value.astype(BF16)

    def shard(k, carry):
        s = 2 * k + core
        slot = x_slot(place, s)
        for pair in range(NB // 2):
            halves = []
            for side in range(2):
                b = index[s, 2 * pair + side]
                x_block = x[slot, pl.ds(block_start(b // BCOLS), BS), :]
                dz_block = dz_t[pl.ds(block_start(b % BCOLS), BS), :]
                halves.append(dot(x_block, dz_block, NT))
            both = jnp.concatenate(halves, axis=1)
            out[k, pair * BS : (pair + 1) * BS, :] = plus(both, k, pair * BS)
        return carry

    lax.fori_loop(0, NK, shard, 0)
    p = jnp.concatenate([p_t[2 * k + core] for k in range(NK)], axis=0)
    for j in range(WIDTH // TOK):
        part = dot(p, dz_t[j * TOK : (j + 1) * TOK, :], NT)
        first = FEAT + j * RS
        for k in range(NK):
            out[k, first : first + RS, :] = plus(part[k * RS : (k + 1) * RS], k, first)


def grad_other_kernel(place, index, x, dz_t, p_t, out):
    grad_rows(place, index, x, dz_t, p_t, out, 1, None)


def grad_own_kernel(place, index, x, dz_t, p_t, other, out):
    grad_rows(place, index, x, dz_t, p_t, out, 0, other)


def u_kernel(place, x, q_t, out):
    q = q_t[place[3]]

    def shard(slot, carry):
        u = dot(q, x[slot], NT).astype(BF16)
        s = x_shard(place, slot)
        for j in range(FEAT // TOK):
            out[s, j * RS : (j + 1) * RS, :] = u[:, j * TOK : (j + 1) * TOK]
        return carry

    lax.fori_loop(0, SH, shard, 0)


def call(kernel, out_shape, flops, bytes_accessed, operands, scratch=(), free=0, scalars=2):
    vmem = pl.BlockSpec(memory_space=pltpu.VMEM)
    smem = pl.BlockSpec(memory_space=pltpu.SMEM)
    anywhere = pl.BlockSpec(memory_space=pl.ANY)
    many = isinstance(out_shape, tuple)
    return pl.pallas_call(
        kernel,
        out_shape=out_shape,
        in_specs=[smem] * scalars + [anywhere] * free + [vmem] * (len(operands) - scalars - free),
        out_specs=(vmem,) * len(out_shape) if many else vmem,
        scratch_shapes=list(scratch),
        compiler_params=pltpu.CompilerParams(vmem_limit_bytes=10 << 20),
        cost_estimate=pl.CostEstimate(
            flops=flops, bytes_accessed=bytes_accessed, transcendentals=0
        ),
    )(*operands)


def shape(*dims, kind=BF16):
    return jax.ShapeDtypeStruct(dims, kind)


def add(*terms):
    return sum(t.astype(F32) for t in terms).astype(BF16)


def shift(x, by):
    return lax.ppermute(x, "z", [(i, (i + by) % NZ) for i in range(NZ)])


def meet(x, axis, flip):
    count = {"z": 8, "xh": 2, "xl": 2, "y": 4, "core": 2}[axis]
    return lax.ppermute(x, axis, [(i, i ^ flip) for i in range(count)])


def on_device(inputs, cotangent, sparse_blocks, block_index, u_factor, v_factor):
    turn = [(r * SH + c, c * SH + r) for r in range(SH) for c in range(SH)]
    place = jnp.stack(
        [lax.axis_index("z"), lax.axis_index("xh"), lax.axis_index("core"), lax.axis_index(ROW)]
    ).astype(jnp.int32)

    w_pairs = sparse_blocks.reshape(NB // 2, 2, BS, BS).transpose(0, 2, 1, 3).reshape(FEAT, 2 * BS)
    index_row = jnp.zeros((16, TOK), BF16).at[0, :NB].set(block_index.reshape(NB).astype(BF16))
    w_mine = jnp.concatenate([w_pairs, index_row])
    w_mine, inputs = lax.optimization_barrier((w_mine, inputs))
    w_all = lax.all_gather(w_mine, COL, axis=0)
    index = w_all[:, FEAT, :NB].astype(jnp.int32)

    mine, p = call(
        first_kernel,
        (shape(FEAT, TOK), shape(RANK, TOK, kind=F32)),
        40_000_000,
        1 << 19,
        (inputs, u_factor),
        scalars=0,
    )
    turned = lax.ppermute(mine, ALL, turn)
    p = p + meet(p, "core", 1)
    turned, p = lax.optimization_barrier((turned, p))
    other, p_in = lax.optimization_barrier((meet(turned, "xh", 1), meet(p, "xl", 1)))
    p = p + p_in
    own = jnp.stack([turned, other])
    held = {0: own}
    for step, flip in ((1, 1), (2, 2), (3, 0)):
        before, after = shift(held[1 - step], 1), shift(held[step - 1], -1)
        p_in = meet(p, "y", flip) if flip else lax.ppermute(p.astype(BF16), ALL, turn)
        held[-step], held[step], p_in = lax.optimization_barrier((before, after, p_in))
        p = p + p_in if flip else p_in
    held[4] = shift(held[-3], 1)
    x_parts = [held[rel if rel <= 4 else rel - NZ] for rel in range(NZ)]

    hidden, dz_t, q, x_all = call(
        forward_kernel,
        (
            shape(TOK, WIDTH),
            shape(WIDTH, TOK),
            shape(RANK, TOK, kind=F32),
            shape(SH, FEAT, TOK),
        ),
        800_000_000,
        10 << 20,
        (place, index, *x_parts, w_all, p, v_factor, cotangent),
        [pltpu.VMEM((WIDTH, TOK), F32), pltpu.SemaphoreType.DMA((NZ,))],
        free=NZ,
    )

    def back_call(slots, dz_back):
        outs = call(
            functools.partial(back_kernel, slots),
            (shape(2, FEAT, TOK),) * (len(slots) // 2),
            20_000_000 * len(slots),
            len(slots) << 19,
            (place, index, w_all, dz_back),
            [pltpu.VMEM((FEAT, TOK), F32), pltpu.VMEM((len(slots), FEAT, TOK), BF16)],
        )
        return {slot // 2 % NZ: part for slot, part in zip(slots[::2], outs)}

    back = back_call(range(6, 12), dz_t)
    dz_t, q, back[3] = lax.optimization_barrier((dz_t, q, back[3]))
    up, down = shift(back[4], 1), shift(back[5], -1)
    q_in = meet(q.astype(BF16), "z", 1)
    back.update(back_call(range(12, 22), dz_t))
    dz_t, q_in, back[0] = lax.optimization_barrier((dz_t, q_in, back[0]))

    q = q + q_in.astype(F32)
    q_in = meet(q.astype(BF16), "z", 2)
    p_slices = p.reshape(SH, RS, TOK)
    grads = call(
        grad_other_kernel,
        shape(NK, FEAT + VROWS, TOK),
        200_000_000,
        4 << 20,
        (place, index, x_all, dz_t, p_slices),
    )
    up, down, q_in, grads = lax.optimization_barrier((up, down, q_in, grads))

    grads_in = meet(grads, "core", 1)
    up, down = shift(add(back[3], up), 1), shift(add(back[6], down), -1)
    q = q + q_in.astype(F32)
    q_in = meet(q.astype(BF16), "z", 4)
    grads = call(
        grad_own_kernel,
        shape(NK, FEAT + VROWS, TOK),
        200_000_000,
        6 << 20,
        (place, index, x_all, dz_t, p_slices, grads_in),
    )
    up, down, q_in, grads = lax.optimization_barrier((up, down, q_in, grads))

    grads_in = lax.all_to_all(grads, ("xl", "y"), 0, 0)
    up, down = shift(add(back[2], up), 1), shift(add(back[7], down), -1)
    q = q + q_in.astype(F32)
    q_in = meet(q.astype(BF16), "xh", 1)
    up, down, q_in = lax.optimization_barrier((up, down, q_in))

    up = shift(add(back[1], up), 1)
    q_t = (q + q_in.astype(F32)).astype(BF16)
    u_part = call(
        u_kernel,
        shape(SH, UROWS, TOK),
        70_000_000,
        3 << 20,
        (place, x_all, q_t.reshape(SH, RS, TOK)),
        scalars=1,
    )
    up, u_part = lax.optimization_barrier((up, u_part))
    other = add(back[0][1], up[1], down[1])
    total = add(back[0][0], up[0], down[0], meet(other, "xh", 1))
    x_grad_t = lax.ppermute(total, ALL, turn)
    q_turned = lax.ppermute(q_t, ALL, turn)
    u_in = lax.all_to_all(u_part, COL, 0, 0)

    grads_sum = jnp.sum(grads_in.astype(F32), axis=0)
    blocks_grad = (
        grads_sum[:FEAT]
        .astype(BF16)
        .reshape(NB // 2, BS, 2, BS)
        .transpose(0, 2, 1, 3)
        .reshape(sparse_blocks.shape)
    )
    v_grad = (
        grads_sum[FEAT:]
        .reshape(WIDTH // TOK, RS, TOK)
        .transpose(1, 0, 2)
        .reshape(RS, WIDTH)
    )
    u_grad = (
        jnp.sum(u_in.astype(F32), axis=0)
        .reshape(FEAT // TOK, RS, TOK)
        .transpose(0, 2, 1)
        .reshape(FEAT, RS)
    )
    x_grad_t, q_turned, blocks_grad, v_grad, u_grad = lax.optimization_barrier(
        (x_grad_t, q_turned, blocks_grad, v_grad, u_grad)
    )
    x_low = lax.dot_general(
        q_turned, u_factor, (((0,), (1,)), ((), ())), preferred_element_type=F32
    )
    input_grad = add(x_grad_t.T, x_low)
    return hidden, input_grad, blocks_grad, u_grad, v_grad


def solution(mesh):
    fine = Mesh(mesh.devices.reshape(8, 2, 2, 4, 2), ALL)
    in_specs = (
        P(ROW, COL),
        P(COL, ROW),
        P(COL, ROW, None, None),
        P(COL, ROW, None),
        P(COL, None),
        P(None, ROW),
    )
    out_specs = (
        P(COL, ROW),
        P(ROW, COL),
        P(COL, ROW, None, None),
        P(COL, ROW),
        P(COL, ROW),
    )
    return jax.shard_map(
        on_device, mesh=fine, in_specs=in_specs, out_specs=out_specs, check_vma=False
    )
```

```python
import functools

import jax
import jax.numpy as jnp
from jax import lax
from jax.experimental import pallas as pl
from jax.experimental.pallas import tpu as pltpu
from jax.sharding import Mesh, PartitionSpec as P

BS = 64
NB = 16
SH = 16
NZ = 8
NK = 8
FEAT = 512
WIDTH = 2048
TOK = 128
RANK = 256
RS = RANK // SH
ROWS = FEAT + RS
WROWS = FEAT + 16
VROWS = WIDTH // TOK * RS
UROWS = FEAT // TOK * RS
BCOLS = WIDTH // BS

ROW = ("z", "xh")
COL = ("xl", "y", "core")
ALL = ROW + COL

NN = (((1,), (0,)), ((), ()))
NT = (((1,), (1,)), ((), ()))
F32 = jnp.float32
BF16 = jnp.bfloat16


def dot(a, b, dims):
    return lax.dot_general(a, b, dims, preferred_element_type=F32)


def gelu_pair(z):
    half = 0.5 * (1.0 + lax.erf(z * 0.7071067811865476))
    slope = half + z * jnp.exp(-0.5 * z * z) * 0.3989422804014327
    return z * half, slope


def block_start(position):
    return pl.multiple_of(position * BS, BS)


def x_slot(place, s):
    return (((s >> 1) - place[0]) & (NZ - 1)) * 2 + ((s & 1) ^ place[1])


def x_shard(place, slot):
    return (((slot >> 1) + place[0]) & (NZ - 1)) * 2 + ((slot & 1) ^ place[1])


def first_kernel(x, u, x_t, p):
    x_t[...] = x[...].T
    p[...] = dot(u[...].T, x_t[...], NN).reshape(SH, RS, TOK)


def forward_kernel(place, index, *refs):
    x_parts = refs[:NZ]
    w, v, cot, hidden, dz_t, q_t, x, z_t, sems = refs[NZ:]
    copies = [
        pltpu.make_async_copy(x_parts[rel], x.at[2 * rel : 2 * rel + 2], sems.at[rel])
        for rel in range(NZ)
    ]
    for copy in copies:
        copy.start()
    z_t[...] = jnp.zeros_like(z_t)
    for copy in copies:
        copy.wait()

    def shard(slot, carry):
        s = x_shard(place, slot)
        sums = []
        for pair in range(NB // 2):
            both = w[s, pair * BS : (pair + 1) * BS, :].T
            for side in range(2):
                b = index[s, 2 * pair + side]
                x_block = x[slot, pl.ds(block_start(b // BCOLS), BS), :]
                sums.append((b % BCOLS, dot(both[side * BS : (side + 1) * BS], x_block, NN)))
        for where, value in sums:
            z_t[pl.ds(block_start(where), BS), :] += value
        return carry

    lax.fori_loop(0, SH, shard, 0)
    p = jnp.concatenate([x[x_slot(place, s), FEAT:, :] for s in range(SH)], axis=0).T
    for j in range(WIDTH // TOK):
        part = slice(j * TOK, (j + 1) * TOK)
        z = z_t[part, :].T + dot(p, v[:, part], NN)
        value, slope = gelu_pair(z)
        hidden[:, part] = value.astype(BF16)
        dz = cot[:, part].astype(F32) * slope
        dz_t[part, :] = dz.T.astype(BF16)
    q_t[...] = dot(v[...], dz_t[...], NN)


def back_kernel(slots, place, index, w, dz_t, *refs):
    outs = refs[: len(slots) // 2]
    total, done = refs[len(slots) // 2 :]

    def shard(i, carry):
        slot = (i + slots[0]) & (2 * NZ - 1)
        s = x_shard(place, slot)
        total[...] = jnp.zeros_like(total)
        sums = []
        for pair in range(NB // 2):
            both = w[s, pair * BS : (pair + 1) * BS, :]
            for side in range(2):
                b = index[s, 2 * pair + side]
                dz_block = dz_t[pl.ds(block_start(b % BCOLS), BS), :]
                sums.append((b // BCOLS, dot(both[:, side * BS : (side + 1) * BS], dz_block, NN)))
        for where, value in sums:
            total[pl.ds(block_start(where), BS), :] += value
        done[i] = total[...].astype(BF16)
        return carry

    lax.fori_loop(0, len(slots), shard, 0)
    for i in range(len(slots) // 2):
        outs[i][...] = done[2 * i : 2 * i + 2]


def grad_rows(place, index, x, dz_t, out, half, other):
    core = place[2] ^ half

    def plus(value, k, first):
        if other is not None:
            value += other[k, first : first + value.shape[0], :].astype(F32)
        return value.astype(BF16)

    def shard(k, carry):
        s = 2 * k + core
        slot = x_slot(place, s)
        for pair in range(NB // 2):
            halves = []
            for side in range(2):
                b = index[s, 2 * pair + side]
                x_block = x[slot, pl.ds(block_start(b // BCOLS), BS), :]
                dz_block = dz_t[pl.ds(block_start(b % BCOLS), BS), :]
                halves.append(dot(x_block, dz_block, NT))
            both = jnp.concatenate(halves, axis=1)
            out[k, pair * BS : (pair + 1) * BS, :] = plus(both, k, pair * BS)
        return carry

    lax.fori_loop(0, NK, shard, 0)
    p = jnp.concatenate([x[x_slot(place, 2 * k + core), FEAT:, :] for k in range(NK)], axis=0)
    for j in range(WIDTH // TOK):
        part = dot(p, dz_t[j * TOK : (j + 1) * TOK, :], NT)
        first = FEAT + j * RS
        for k in range(NK):
            out[k, first : first + RS, :] = plus(part[k * RS : (k + 1) * RS], k, first)


def grad_other_kernel(place, index, x, dz_t, out):
    grad_rows(place, index, x, dz_t, out, 1, None)


def grad_own_kernel(place, index, x, dz_t, q_t, other, out):
    grad_rows(place, index, x, dz_t, out, 0, other)
    q = q_t[place[3]]

    def shard(k, carry):
        for half in range(2):
            slot = x_slot(place, 2 * k + (place[2] ^ half))
            u = dot(q, x[slot, :FEAT, :], NT).astype(BF16)
            for j in range(FEAT // TOK):
                first = FEAT + VROWS + half * UROWS + j * RS
                out[k, first : first + RS, :] = u[:, j * TOK : (j + 1) * TOK]
        return carry

    lax.fori_loop(0, NK, shard, 0)


def call(kernel, out_shape, flops, bytes_accessed, operands, scratch=(), free=0, scalars=2):
    vmem = pl.BlockSpec(memory_space=pltpu.VMEM)
    smem = pl.BlockSpec(memory_space=pltpu.SMEM)
    anywhere = pl.BlockSpec(memory_space=pl.ANY)
    many = isinstance(out_shape, tuple)
    return pl.pallas_call(
        kernel,
        out_shape=out_shape,
        in_specs=[smem] * scalars + [anywhere] * free + [vmem] * (len(operands) - scalars - free),
        out_specs=(vmem,) * len(out_shape) if many else vmem,
        scratch_shapes=list(scratch),
        compiler_params=pltpu.CompilerParams(vmem_limit_bytes=10 << 20),
        cost_estimate=pl.CostEstimate(
            flops=flops, bytes_accessed=bytes_accessed, transcendentals=0
        ),
    )(*operands)


def shape(*dims, kind=BF16):
    return jax.ShapeDtypeStruct(dims, kind)


def add(*terms):
    return sum(t.astype(F32) for t in terms).astype(BF16)


def shift(x, by):
    return lax.ppermute(x, "z", [(i, (i + by) % NZ) for i in range(NZ)])


def meet(x, axis, flip):
    count = {"z": 8, "xh": 2, "xl": 2, "y": 4, "core": 2}[axis]
    return lax.ppermute(x, axis, [(i, i ^ flip) for i in range(count)])


def on_device(inputs, cotangent, sparse_blocks, block_index, u_factor, v_factor):
    turn = [(r * SH + c, c * SH + r) for r in range(SH) for c in range(SH)]
    turn_pair = [(r * SH + c, (c ^ 1) * SH + r) for r in range(SH) for c in range(SH)]
    place = jnp.stack(
        [lax.axis_index("z"), lax.axis_index("xh"), lax.axis_index("core"), lax.axis_index(ROW)]
    ).astype(jnp.int32)

    w_pairs = sparse_blocks.reshape(NB // 2, 2, BS, BS).transpose(0, 2, 1, 3).reshape(FEAT, 2 * BS)
    index_row = jnp.zeros((16, TOK), BF16).at[0, :NB].set(block_index.reshape(NB).astype(BF16))
    w_mine = jnp.concatenate([w_pairs, index_row])
    w_mine, inputs = lax.optimization_barrier((w_mine, inputs))
    w_all = lax.all_gather(w_mine, COL, axis=0)

    mine, p = call(
        first_kernel,
        (shape(FEAT, TOK), shape(SH, RS, TOK, kind=F32)),
        40_000_000,
        1 << 19,
        (inputs, u_factor),
        scalars=0,
    )
    turned = lax.ppermute(mine, ALL, turn)
    p_in = lax.all_to_all(p, COL, 0, 0)
    turned, p_in = lax.optimization_barrier((turned, p_in))
    p = jnp.sum(p_in, axis=0).astype(BF16)
    parts = [
        turned,
        lax.ppermute(p, ALL, turn),
        meet(turned, "xh", 1),
        lax.ppermute(p, ALL, turn_pair),
    ]
    held = {0: jnp.concatenate(parts).reshape(2, ROWS, TOK)}
    for step in (1, 2, 3):
        held[-step], held[step] = shift(held[1 - step], 1), shift(held[step - 1], -1)
        if step == 2:
            w_all, held[-2], held[2] = lax.optimization_barrier((w_all, held[-2], held[2]))
    held[4] = shift(held[-3], 1)
    x_parts = [held[rel if rel <= 4 else rel - NZ] for rel in range(NZ)]
    index = w_all[:, FEAT, :NB].astype(jnp.int32)

    hidden, dz_t, q, x_all = call(
        forward_kernel,
        (
            shape(TOK, WIDTH),
            shape(WIDTH, TOK),
            shape(RANK, TOK, kind=F32),
            shape(SH, ROWS, TOK),
        ),
        800_000_000,
        10 << 20,
        (place, index, *x_parts, w_all, v_factor, cotangent),
        [pltpu.VMEM((WIDTH, TOK), F32), pltpu.SemaphoreType.DMA((NZ,))],
        free=NZ,
    )

    def back_call(slots, dz_back):
        outs = call(
            functools.partial(back_kernel, slots),
            (shape(2, FEAT, TOK),) * (len(slots) // 2),
            20_000_000 * len(slots),
            len(slots) << 19,
            (place, index, w_all, dz_back),
            [pltpu.VMEM((FEAT, TOK), F32), pltpu.VMEM((len(slots), FEAT, TOK), BF16)],
        )
        return {slot // 2 % NZ: part for slot, part in zip(slots[::2], outs)}

    q_in = meet(q.astype(BF16), "z", 1)
    back = back_call(range(6, 12), dz_t)
    dz_t, q_in, back[3] = lax.optimization_barrier((dz_t, q_in, back[3]))

    up, down = shift(back[4], 1), shift(back[5], -1)
    q = q + q_in.astype(F32)
    q_in = meet(q.astype(BF16), "z", 2)
    back.update(back_call(range(12, 22), dz_t))
    dz_t, q_in, back[0] = lax.optimization_barrier((dz_t, q_in, back[0]))

    q = q + q_in.astype(F32)
    q_in = meet(q.astype(BF16), "z", 4)
    grads = call(
        grad_other_kernel,
        shape(NK, FEAT + VROWS, TOK),
        200_000_000,
        4 << 20,
        (place, index, x_all, dz_t),
    )
    up, down, q_in, grads = lax.optimization_barrier((up, down, q_in, grads))

    grads_in = meet(grads, "core", 1)
    up, down = shift(add(back[3], up), 1), shift(add(back[6], down), -1)
    q = q + q_in.astype(F32)
    q_in = meet(q.astype(BF16), "xh", 1)
    up, down, q_in, grads_in = lax.optimization_barrier((up, down, q_in, grads_in))

    up, down = shift(add(back[2], up), 1), shift(add(back[7], down), -1)
    q_t = (q + q_in.astype(F32)).astype(BF16)
    grads = call(
        grad_own_kernel,
        shape(NK, FEAT + VROWS + 2 * UROWS, TOK),
        300_000_000,
        6 << 20,
        (place, index, x_all, dz_t, q_t.reshape(SH, RS, TOK), grads_in),
    )
    up, down, grads = lax.optimization_barrier((up, down, grads))

    up = shift(add(back[1], up), 1)
    other = add(back[0][1], up[1], down[1])
    total = add(back[0][0], up[0], down[0], meet(other, "xh", 1))
    x_grad_t = lax.ppermute(total, ALL, turn)
    grads_in = lax.all_to_all(grads, ("xl", "y"), 0, 0)
    q_turned = lax.ppermute(q_t, ALL, turn)

    grads_sum = jnp.sum(grads_in.astype(F32), axis=0)
    blocks_grad = (
        grads_sum[:FEAT]
        .astype(BF16)
        .reshape(NB // 2, BS, 2, BS)
        .transpose(0, 2, 1, 3)
        .reshape(sparse_blocks.shape)
    )
    v_grad = (
        grads_sum[FEAT : FEAT + VROWS]
        .reshape(WIDTH // TOK, RS, TOK)
        .transpose(1, 0, 2)
        .reshape(RS, WIDTH)
    )
    u_own = grads_sum[FEAT + VROWS : FEAT + VROWS + UROWS]
    u_other = grads_sum[FEAT + VROWS + UROWS :]
    u_grad = (
        (u_own + meet(u_other, "core", 1))
        .reshape(FEAT // TOK, RS, TOK)
        .transpose(0, 2, 1)
        .reshape(FEAT, RS)
    )
    x_grad_t, q_turned, blocks_grad, v_grad, u_grad = lax.optimization_barrier(
        (x_grad_t, q_turned, blocks_grad, v_grad, u_grad)
    )
    x_low = lax.dot_general(
        q_turned, u_factor, (((0,), (1,)), ((), ())), preferred_element_type=F32
    )
    input_grad = add(x_grad_t.T, x_low)
    return hidden, input_grad, blocks_grad, u_grad, v_grad


def solution(mesh):
    fine = Mesh(mesh.devices.reshape(8, 2, 2, 4, 2), ALL)
    in_specs = (
        P(ROW, COL),
        P(COL, ROW),
        P(COL, ROW, None, None),
        P(COL, ROW, None),
        P(COL, None),
        P(None, ROW),
    )
    out_specs = (
        P(COL, ROW),
        P(ROW, COL),
        P(COL, ROW, None, None),
        P(COL, ROW),
        P(COL, ROW),
    )
    return jax.shard_map(
        on_device, mesh=fine, in_specs=in_specs, out_specs=out_specs, check_vma=False
    )
```

```python
import functools

import jax
import jax.numpy as jnp
from jax import lax
from jax.experimental import pallas as pl
from jax.experimental.pallas import tpu as pltpu
from jax.sharding import Mesh, PartitionSpec as P

BS = 64
NB = 16
SH = 16
NZ = 8
NK = 8
FEAT = 512
WIDTH = 2048
TOK = 128
RANK = 256
RS = RANK // SH
ROWS = FEAT + RS
WROWS = FEAT + 16
VROWS = WIDTH // TOK * RS
UROWS = FEAT // TOK * RS
BCOLS = WIDTH // BS

ROW = ("z", "xh")
COL = ("xl", "y", "core")
ALL = ROW + COL

NN = (((1,), (0,)), ((), ()))
NT = (((1,), (1,)), ((), ()))
F32 = jnp.float32
BF16 = jnp.bfloat16


def dot(a, b, dims):
    return lax.dot_general(a, b, dims, preferred_element_type=F32)


def gelu_pair(z):
    half = 0.5 * (1.0 + lax.erf(z * 0.7071067811865476))
    slope = half + z * jnp.exp(-0.5 * z * z) * 0.3989422804014327
    return z * half, slope


def block_start(position):
    return pl.multiple_of(position * BS, BS)


def x_slot(place, s):
    return (((s >> 1) - place[0]) & (NZ - 1)) * 2 + ((s & 1) ^ place[1])


def x_shard(place, slot):
    return (((slot >> 1) + place[0]) & (NZ - 1)) * 2 + ((slot & 1) ^ place[1])


def first_kernel(x, u, x_t, p):
    x_t[...] = x[...].T
    whole = dot(u[...].T, x_t[...], NN)
    for s in range(SH):
        for j in range(2):
            p[s, j] = whole[(s ^ j) * RS : (s ^ j) * RS + RS]


def forward_kernel(place, index, *refs):
    x_parts = refs[:NZ]
    w, v, cot, hidden, dz_t, q_t, x, z_t, sems = refs[NZ:]
    copies = [
        pltpu.make_async_copy(x_parts[rel], x.at[2 * rel : 2 * rel + 2], sems.at[rel])
        for rel in range(NZ)
    ]
    for copy in copies:
        copy.start()
    z_t[...] = jnp.zeros_like(z_t)
    for copy in copies:
        copy.wait()

    def shard(slot, carry):
        s = x_shard(place, slot)
        sums = []
        for pair in range(NB // 2):
            both = w[s, pair * BS : (pair + 1) * BS, :].T
            for side in range(2):
                b = index[s, 2 * pair + side]
                x_block = x[slot, pl.ds(block_start(b // BCOLS), BS), :]
                sums.append((b % BCOLS, dot(both[side * BS : (side + 1) * BS], x_block, NN)))
        for where, value in sums:
            z_t[pl.ds(block_start(where), BS), :] += value
        return carry

    lax.fori_loop(0, SH, shard, 0)
    p = jnp.concatenate([x[x_slot(place, s), FEAT:, :] for s in range(SH)], axis=0).T
    for j in range(WIDTH // TOK):
        part = slice(j * TOK, (j + 1) * TOK)
        z = z_t[part, :].T + dot(p, v[:, part], NN)
        value, slope = gelu_pair(z)
        hidden[:, part] = value.astype(BF16)
        dz = cot[:, part].astype(F32) * slope
        dz_t[part, :] = dz.T.astype(BF16)
    q_t[...] = dot(v[...], dz_t[...], NN)


def back_kernel(slots, place, index, w, dz_t, *refs):
    outs = refs[: len(slots) // 2]
    total, done = refs[len(slots) // 2 :]

    def shard(i, carry):
        slot = (i + slots[0]) & (2 * NZ - 1)
        s = x_shard(place, slot)
        total[...] = jnp.zeros_like(total)
        sums = []
        for pair in range(NB // 2):
            both = w[s, pair * BS : (pair + 1) * BS, :]
            for side in range(2):
                b = index[s, 2 * pair + side]
                dz_block = dz_t[pl.ds(block_start(b % BCOLS), BS), :]
                sums.append((b // BCOLS, dot(both[:, side * BS : (side + 1) * BS], dz_block, NN)))
        for where, value in sums:
            total[pl.ds(block_start(where), BS), :] += value
        done[i] = total[...].astype(BF16)
        return carry

    lax.fori_loop(0, len(slots), shard, 0)
    for i in range(len(slots) // 2):
        outs[i][...] = done[2 * i : 2 * i + 2]


def grad_rows(place, index, x, dz_t, out, half, other):
    core = place[2] ^ half

    def plus(value, k, first):
        if other is not None:
            value += other[k, first : first + value.shape[0], :].astype(F32)
        return value.astype(BF16)

    def shard(k, carry):
        s = 2 * k + core
        slot = x_slot(place, s)
        for pair in range(NB // 2):
            halves = []
            for side in range(2):
                b = index[s, 2 * pair + side]
                x_block = x[slot, pl.ds(block_start(b // BCOLS), BS), :]
                dz_block = dz_t[pl.ds(block_start(b % BCOLS), BS), :]
                halves.append(dot(x_block, dz_block, NT))
            both = jnp.concatenate(halves, axis=1)
            out[k, pair * BS : (pair + 1) * BS, :] = plus(both, k, pair * BS)
        return carry

    lax.fori_loop(0, NK, shard, 0)
    p = jnp.concatenate([x[x_slot(place, 2 * k + core), FEAT:, :] for k in range(NK)], axis=0)
    for j in range(WIDTH // TOK):
        part = dot(p, dz_t[j * TOK : (j + 1) * TOK, :], NT)
        first = FEAT + j * RS
        for k in range(NK):
            out[k, first : first + RS, :] = plus(part[k * RS : (k + 1) * RS], k, first)


def grad_other_kernel(place, index, x, dz_t, out):
    grad_rows(place, index, x, dz_t, out, 1, None)


def grad_own_kernel(place, index, x, dz_t, other, out):
    grad_rows(place, index, x, dz_t, out, 0, other)


def u_kernel(place, grads, x, q_t, out, rows, sem):
    q = q_t[place[3]]

    def shard(k, carry):
        for half in range(2):
            slot = x_slot(place, 2 * k + (place[2] ^ half))
            u = dot(q, x[slot, :FEAT, :], NT).astype(BF16)
            for j in range(FEAT // TOK):
                first = half * UROWS + j * RS
                rows[k, first : first + RS, :] = u[:, j * TOK : (j + 1) * TOK]
        return carry

    lax.fori_loop(0, NK, shard, 0)
    copy = pltpu.make_async_copy(rows, out.at[:, FEAT + VROWS :, :], sem)
    copy.start()
    copy.wait()


def u_call(place, grads, x, q_t):
    vmem = pl.BlockSpec(memory_space=pltpu.VMEM)
    anywhere = pl.BlockSpec(memory_space=pl.ANY)
    return pl.pallas_call(
        u_kernel,
        out_shape=jax.ShapeDtypeStruct(grads.shape, BF16),
        in_specs=[pl.BlockSpec(memory_space=pltpu.SMEM), anywhere, vmem, vmem],
        out_specs=anywhere,
        scratch_shapes=[pltpu.VMEM((NK, 2 * UROWS, TOK), BF16), pltpu.SemaphoreType.DMA],
        input_output_aliases={1: 0},
        compiler_params=pltpu.CompilerParams(vmem_limit_bytes=10 << 20),
        cost_estimate=pl.CostEstimate(
            flops=70_000_000, bytes_accessed=3 << 20, transcendentals=0
        ),
    )(place, grads, x, q_t)


def call(kernel, out_shape, flops, bytes_accessed, operands, scratch=(), free=0, scalars=2):
    vmem = pl.BlockSpec(memory_space=pltpu.VMEM)
    smem = pl.BlockSpec(memory_space=pltpu.SMEM)
    anywhere = pl.BlockSpec(memory_space=pl.ANY)
    many = isinstance(out_shape, tuple)
    return pl.pallas_call(
        kernel,
        out_shape=out_shape,
        in_specs=[smem] * scalars + [anywhere] * free + [vmem] * (len(operands) - scalars - free),
        out_specs=(vmem,) * len(out_shape) if many else vmem,
        scratch_shapes=list(scratch),
        compiler_params=pltpu.CompilerParams(vmem_limit_bytes=10 << 20),
        cost_estimate=pl.CostEstimate(
            flops=flops, bytes_accessed=bytes_accessed, transcendentals=0
        ),
    )(*operands)


def shape(*dims, kind=BF16):
    return jax.ShapeDtypeStruct(dims, kind)


def add(*terms):
    return sum(t.astype(F32) for t in terms).astype(BF16)


def shift(x, by):
    return lax.ppermute(x, "z", [(i, (i + by) % NZ) for i in range(NZ)])


def meet(x, axis, flip):
    count = {"z": 8, "xh": 2, "xl": 2, "y": 4, "core": 2}[axis]
    return lax.ppermute(x, axis, [(i, i ^ flip) for i in range(count)])


def on_device(inputs, cotangent, sparse_blocks, block_index, u_factor, v_factor):
    turn = [(r * SH + c, c * SH + r) for r in range(SH) for c in range(SH)]
    place = jnp.stack(
        [lax.axis_index("z"), lax.axis_index("xh"), lax.axis_index("core"), lax.axis_index(ROW)]
    ).astype(jnp.int32)

    w_pairs = sparse_blocks.reshape(NB // 2, 2, BS, BS).transpose(0, 2, 1, 3).reshape(FEAT, 2 * BS)
    index_row = jnp.zeros((16, TOK), BF16).at[0, :NB].set(block_index.reshape(NB).astype(BF16))
    w_mine = jnp.concatenate([w_pairs, index_row])
    w_mine, inputs = lax.optimization_barrier((w_mine, inputs))
    w_all = lax.all_gather(w_mine, COL, axis=0)

    mine, p = call(
        first_kernel,
        (shape(FEAT, TOK), shape(SH, 2, RS, TOK, kind=F32)),
        40_000_000,
        1 << 19,
        (inputs, u_factor),
        scalars=0,
    )
    turned = lax.ppermute(mine, ALL, turn)
    p_in = lax.all_to_all(p, COL, 0, 0)
    turned, p_in = lax.optimization_barrier((turned, p_in))
    p = lax.ppermute(jnp.sum(p_in, axis=0).astype(BF16), ALL, turn)
    parts = [turned, p[0], meet(turned, "xh", 1), p[1]]
    held = {0: jnp.concatenate(parts).reshape(2, ROWS, TOK)}
    for step in (1, 2, 3):
        held[-step], held[step] = shift(held[1 - step], 1), shift(held[step - 1], -1)
        if step == 2:
            w_all, held[-2], held[2] = lax.optimization_barrier((w_all, held[-2], held[2]))
    held[4] = shift(held[-3], 1)
    x_parts = [held[rel if rel <= 4 else rel - NZ] for rel in range(NZ)]
    index = w_all[:, FEAT, :NB].astype(jnp.int32)

    hidden, dz_t, q, x_all = call(
        forward_kernel,
        (
            shape(TOK, WIDTH),
            shape(WIDTH, TOK),
            shape(RANK, TOK, kind=F32),
            shape(SH, ROWS, TOK),
        ),
        800_000_000,
        10 << 20,
        (place, index, *x_parts, w_all, v_factor, cotangent),
        [pltpu.VMEM((WIDTH, TOK), F32), pltpu.SemaphoreType.DMA((NZ,))],
        free=NZ,
    )

    def back_call(slots, dz_back):
        outs = call(
            functools.partial(back_kernel, slots),
            (shape(2, FEAT, TOK),) * (len(slots) // 2),
            20_000_000 * len(slots),
            len(slots) << 19,
            (place, index, w_all, dz_back),
            [pltpu.VMEM((FEAT, TOK), F32), pltpu.VMEM((len(slots), FEAT, TOK), BF16)],
        )
        return {slot // 2 % NZ: part for slot, part in zip(slots[::2], outs)}

    q_in = meet(q.astype(BF16), "z", 1)
    back = back_call(range(6, 12), dz_t)
    dz_t, q_in, back[3] = lax.optimization_barrier((dz_t, q_in, back[3]))

    up, down = shift(back[4], 1), shift(back[5], -1)
    q = q + q_in.astype(F32)
    q_in = meet(q.astype(BF16), "z", 2)
    back.update(back_call(range(12, 22), dz_t))
    dz_t, q_in, back[0] = lax.optimization_barrier((dz_t, q_in, back[0]))

    q = q + q_in.astype(F32)
    q_in = meet(q.astype(BF16), "z", 4)
    grads = call(
        grad_other_kernel,
        shape(NK, FEAT + VROWS, TOK),
        200_000_000,
        4 << 20,
        (place, index, x_all, dz_t),
    )
    up, down, q_in, grads = lax.optimization_barrier((up, down, q_in, grads))

    grads_in = meet(grads, "core", 1)
    up, down = shift(add(back[3], up), 1), shift(add(back[6], down), -1)
    q = q + q_in.astype(F32)
    q_in = meet(q.astype(BF16), "xh", 1)
    grads = call(
        grad_own_kernel,
        shape(NK, FEAT + VROWS + 2 * UROWS, TOK),
        200_000_000,
        6 << 20,
        (place, index, x_all, dz_t, grads_in),
    )
    up, down, q_in, grads = lax.optimization_barrier((up, down, q_in, grads))

    up, down = shift(add(back[2], up), 1), shift(add(back[7], down), -1)
    q_t = (q + q_in.astype(F32)).astype(BF16)
    grads = u_call(place, grads, x_all, q_t.reshape(SH, RS, TOK))
    up, down, grads, q_t = lax.optimization_barrier((up, down, grads, q_t))

    up = shift(add(back[1], up), 1)
    other = add(back[0][1], up[1], down[1])
    total = add(back[0][0], up[0], down[0], meet(other, "xh", 1))
    x_grad_t = lax.ppermute(total, ALL, turn)
    grads_in = lax.all_to_all(grads, ("xl", "y"), 0, 0)
    q_turned = lax.ppermute(q_t, ALL, turn)

    grads_sum = jnp.sum(grads_in.astype(F32), axis=0)
    blocks_grad = (
        grads_sum[:FEAT]
        .astype(BF16)
        .reshape(NB // 2, BS, 2, BS)
        .transpose(0, 2, 1, 3)
        .reshape(sparse_blocks.shape)
    )
    v_grad = (
        grads_sum[FEAT : FEAT + VROWS]
        .reshape(WIDTH // TOK, RS, TOK)
        .transpose(1, 0, 2)
        .reshape(RS, WIDTH)
    )
    u_own = grads_sum[FEAT + VROWS : FEAT + VROWS + UROWS]
    u_other = grads_sum[FEAT + VROWS + UROWS :]
    u_grad = (
        (u_own + meet(u_other, "core", 1))
        .reshape(FEAT // TOK, RS, TOK)
        .transpose(0, 2, 1)
        .reshape(FEAT, RS)
    )
    x_grad_t, q_turned, blocks_grad, v_grad, u_grad = lax.optimization_barrier(
        (x_grad_t, q_turned, blocks_grad, v_grad, u_grad)
    )
    x_low = lax.dot_general(
        q_turned, u_factor, (((0,), (1,)), ((), ())), preferred_element_type=F32
    )
    input_grad = add(x_grad_t.T, x_low)
    return hidden, input_grad, blocks_grad, u_grad, v_grad


def solution(mesh):
    fine = Mesh(mesh.devices.reshape(8, 2, 2, 4, 2), ALL)
    in_specs = (
        P(ROW, COL),
        P(COL, ROW),
        P(COL, ROW, None, None),
        P(COL, ROW, None),
        P(COL, None),
        P(None, ROW),
    )
    out_specs = (
        P(COL, ROW),
        P(ROW, COL),
        P(COL, ROW, None, None),
        P(COL, ROW),
        P(COL, ROW),
    )
    return jax.shard_map(
        on_device, mesh=fine, in_specs=in_specs, out_specs=out_specs, check_vma=False
    )
```

```python
import functools

import jax
import jax.numpy as jnp
from jax import lax
from jax.experimental import pallas as pl
from jax.experimental.pallas import tpu as pltpu
from jax.sharding import Mesh, PartitionSpec as P

BS = 64
NB = 16
SH = 16
NZ = 8
NK = 8
FEAT = 512
WIDTH = 2048
TOK = 128
RANK = 256
RS = RANK // SH
ROWS = FEAT + RS
WROWS = FEAT + 16
VROWS = WIDTH // TOK * RS
UROWS = FEAT // TOK * RS
BCOLS = WIDTH // BS

ROW = ("z", "xh")
COL = ("xl", "y", "core")
ALL = ROW + COL

NN = (((1,), (0,)), ((), ()))
NT = (((1,), (1,)), ((), ()))
F32 = jnp.float32
BF16 = jnp.bfloat16


def dot(a, b, dims):
    return lax.dot_general(a, b, dims, preferred_element_type=F32)


def gelu_pair(z):
    half = 0.5 * (1.0 + lax.erf(z * 0.7071067811865476))
    slope = half + z * jnp.exp(-0.5 * z * z) * 0.3989422804014327
    return z * half, slope


def block_start(position):
    return pl.multiple_of(position * BS, BS)


def x_slot(place, s):
    return (((s >> 1) - place[0]) & (NZ - 1)) * 2 + ((s & 1) ^ place[1])


def x_shard(place, slot):
    return (((slot >> 1) + place[0]) & (NZ - 1)) * 2 + ((slot & 1) ^ place[1])


def first_kernel(x, u, x_t, p):
    x_t[...] = x[...].T
    p[...] = dot(u[...].T, x_t[...], NN).reshape(SH, RS, TOK)


def forward_kernel(place, index, *refs):
    x_parts = refs[:NZ]
    w, v, cot, hidden, dz_t, q_t, x, z_t, sems = refs[NZ:]
    copies = [
        pltpu.make_async_copy(x_parts[rel], x.at[2 * rel : 2 * rel + 2], sems.at[rel])
        for rel in range(NZ)
    ]
    for copy in copies:
        copy.start()
    z_t[...] = jnp.zeros_like(z_t)
    for copy in copies:
        copy.wait()

    def shard(slot, carry):
        s = x_shard(place, slot)
        sums = []
        for pair in range(NB // 2):
            both = w[s, pair * BS : (pair + 1) * BS, :].T
            for side in range(2):
                b = index[s, 2 * pair + side]
                x_block = x[slot, pl.ds(block_start(b // BCOLS), BS), :]
                sums.append((b % BCOLS, dot(both[side * BS : (side + 1) * BS], x_block, NN)))
        for where, value in sums:
            z_t[pl.ds(block_start(where), BS), :] += value
        return carry

    lax.fori_loop(0, SH, shard, 0)
    p = jnp.concatenate([x[x_slot(place, s), FEAT:, :] for s in range(SH)], axis=0).T
    for j in range(WIDTH // TOK):
        part = slice(j * TOK, (j + 1) * TOK)
        z = z_t[part, :].T + dot(p, v[:, part], NN)
        value, slope = gelu_pair(z)
        hidden[:, part] = value.astype(BF16)
        dz = cot[:, part].astype(F32) * slope
        dz_t[part, :] = dz.T.astype(BF16)
    q_t[...] = dot(v[...], dz_t[...], NN)


def back_kernel(slots, place, index, w, dz_t, *refs):
    outs = refs[: len(slots) // 2]
    total, done = refs[len(slots) // 2 :]

    def shard(i, carry):
        slot = (i + slots[0]) & (2 * NZ - 1)
        s = x_shard(place, slot)
        total[...] = jnp.zeros_like(total)
        sums = []
        for pair in range(NB // 2):
            both = w[s, pair * BS : (pair + 1) * BS, :]
            for side in range(2):
                b = index[s, 2 * pair + side]
                dz_block = dz_t[pl.ds(block_start(b % BCOLS), BS), :]
                sums.append((b // BCOLS, dot(both[:, side * BS : (side + 1) * BS], dz_block, NN)))
        for where, value in sums:
            total[pl.ds(block_start(where), BS), :] += value
        done[i] = total[...].astype(BF16)
        return carry

    lax.fori_loop(0, len(slots), shard, 0)
    for i in range(len(slots) // 2):
        outs[i][...] = done[2 * i : 2 * i + 2]


def grad_rows(place, index, x, dz_t, out, half, other):
    core = place[2] ^ half

    def plus(value, k, first):
        if other is not None:
            value += other[k, first : first + value.shape[0], :].astype(F32)
        return value.astype(BF16)

    def shard(k, carry):
        s = 2 * k + core
        slot = x_slot(place, s)
        for pair in range(NB // 2):
            halves = []
            for side in range(2):
                b = index[s, 2 * pair + side]
                x_block = x[slot, pl.ds(block_start(b // BCOLS), BS), :]
                dz_block = dz_t[pl.ds(block_start(b % BCOLS), BS), :]
                halves.append(dot(x_block, dz_block, NT))
            both = jnp.concatenate(halves, axis=1)
            out[k, pair * BS : (pair + 1) * BS, :] = plus(both, k, pair * BS)
        return carry

    lax.fori_loop(0, NK, shard, 0)
    p = jnp.concatenate([x[x_slot(place, 2 * k + core), FEAT:, :] for k in range(NK)], axis=0)
    for j in range(WIDTH // TOK):
        part = dot(p, dz_t[j * TOK : (j + 1) * TOK, :], NT)
        first = FEAT + j * RS
        for k in range(NK):
            out[k, first : first + RS, :] = plus(part[k * RS : (k + 1) * RS], k, first)


def grad_other_kernel(place, index, x, dz_t, out):
    grad_rows(place, index, x, dz_t, out, 1, None)


def grad_own_kernel(place, index, x, dz_t, other, out):
    grad_rows(place, index, x, dz_t, out, 0, other)


def u_kernel(place, grads, x, q_t, out, rows, sem):
    q = q_t[place[3]]

    def shard(k, carry):
        for half in range(2):
            slot = x_slot(place, 2 * k + (place[2] ^ half))
            u = dot(q, x[slot, :FEAT, :], NT).astype(BF16)
            for j in range(FEAT // TOK):
                first = half * UROWS + j * RS
                rows[k, first : first + RS, :] = u[:, j * TOK : (j + 1) * TOK]
        return carry

    lax.fori_loop(0, NK, shard, 0)
    copy = pltpu.make_async_copy(rows, out.at[:, FEAT + VROWS :, :], sem)
    copy.start()
    copy.wait()


def u_call(place, grads, x, q_t):
    vmem = pl.BlockSpec(memory_space=pltpu.VMEM)
    anywhere = pl.BlockSpec(memory_space=pl.ANY)
    return pl.pallas_call(
        u_kernel,
        out_shape=jax.ShapeDtypeStruct(grads.shape, BF16),
        in_specs=[pl.BlockSpec(memory_space=pltpu.SMEM), anywhere, vmem, vmem],
        out_specs=anywhere,
        scratch_shapes=[pltpu.VMEM((NK, 2 * UROWS, TOK), BF16), pltpu.SemaphoreType.DMA],
        input_output_aliases={1: 0},
        compiler_params=pltpu.CompilerParams(vmem_limit_bytes=10 << 20),
        cost_estimate=pl.CostEstimate(
            flops=70_000_000, bytes_accessed=3 << 20, transcendentals=0
        ),
    )(place, grads, x, q_t)


def call(kernel, out_shape, flops, bytes_accessed, operands, scratch=(), free=0, scalars=2):
    vmem = pl.BlockSpec(memory_space=pltpu.VMEM)
    smem = pl.BlockSpec(memory_space=pltpu.SMEM)
    anywhere = pl.BlockSpec(memory_space=pl.ANY)
    many = isinstance(out_shape, tuple)
    return pl.pallas_call(
        kernel,
        out_shape=out_shape,
        in_specs=[smem] * scalars + [anywhere] * free + [vmem] * (len(operands) - scalars - free),
        out_specs=(vmem,) * len(out_shape) if many else vmem,
        scratch_shapes=list(scratch),
        compiler_params=pltpu.CompilerParams(vmem_limit_bytes=10 << 20),
        cost_estimate=pl.CostEstimate(
            flops=flops, bytes_accessed=bytes_accessed, transcendentals=0
        ),
    )(*operands)


def shape(*dims, kind=BF16):
    return jax.ShapeDtypeStruct(dims, kind)


def add(*terms):
    return sum(t.astype(F32) for t in terms).astype(BF16)


def shift(x, by):
    return lax.ppermute(x, "z", [(i, (i + by) % NZ) for i in range(NZ)])


def meet(x, axis, flip):
    count = {"z": 8, "xh": 2, "xl": 2, "y": 4, "core": 2}[axis]
    return lax.ppermute(x, axis, [(i, i ^ flip) for i in range(count)])


def on_device(inputs, cotangent, sparse_blocks, block_index, u_factor, v_factor):
    turn = [(r * SH + c, c * SH + r) for r in range(SH) for c in range(SH)]
    turn_pair = [(r * SH + c, (c ^ 1) * SH + r) for r in range(SH) for c in range(SH)]
    place = jnp.stack(
        [lax.axis_index("z"), lax.axis_index("xh"), lax.axis_index("core"), lax.axis_index(ROW)]
    ).astype(jnp.int32)

    w_pairs = sparse_blocks.reshape(NB // 2, 2, BS, BS).transpose(0, 2, 1, 3).reshape(FEAT, 2 * BS)
    index_row = jnp.zeros((16, TOK), BF16).at[0, :NB].set(block_index.reshape(NB).astype(BF16))
    w_mine = jnp.concatenate([w_pairs, index_row])
    w_mine, inputs = lax.optimization_barrier((w_mine, inputs))
    w_all = lax.all_gather(w_mine, COL, axis=0)

    mine, p = call(
        first_kernel,
        (shape(FEAT, TOK), shape(SH, RS, TOK, kind=F32)),
        40_000_000,
        1 << 19,
        (inputs, u_factor),
        scalars=0,
    )
    turned = lax.ppermute(mine, ALL, turn)
    p_in = lax.all_to_all(p, COL, 0, 0)
    turned, p_in = lax.optimization_barrier((turned, p_in))
    p = jnp.sum(p_in, axis=0).astype(BF16)
    parts = [
        turned,
        lax.ppermute(p, ALL, turn),
        meet(turned, "xh", 1),
        lax.ppermute(p, ALL, turn_pair),
    ]
    held = {0: jnp.concatenate(parts).reshape(2, ROWS, TOK)}
    for step in (1, 2, 3):
        held[-step], held[step] = shift(held[1 - step], 1), shift(held[step - 1], -1)
        if step == 2:
            w_all, held[-2], held[2] = lax.optimization_barrier((w_all, held[-2], held[2]))
    held[4] = shift(held[-3], 1)
    x_parts = [held[rel if rel <= 4 else rel - NZ] for rel in range(NZ)]
    index = w_all[:, FEAT, :NB].astype(jnp.int32)

    hidden, dz_t, q, x_all = call(
        forward_kernel,
        (
            shape(TOK, WIDTH),
            shape(WIDTH, TOK),
            shape(RANK, TOK, kind=F32),
            shape(SH, ROWS, TOK),
        ),
        800_000_000,
        10 << 20,
        (place, index, *x_parts, w_all, v_factor, cotangent),
        [pltpu.VMEM((WIDTH, TOK), F32), pltpu.SemaphoreType.DMA((NZ,))],
        free=NZ,
    )

    def back_call(slots, dz_back):
        outs = call(
            functools.partial(back_kernel, slots),
            (shape(2, FEAT, TOK),) * (len(slots) // 2),
            20_000_000 * len(slots),
            len(slots) << 19,
            (place, index, w_all, dz_back),
            [pltpu.VMEM((FEAT, TOK), F32), pltpu.VMEM((len(slots), FEAT, TOK), BF16)],
        )
        return {slot // 2 % NZ: part for slot, part in zip(slots[::2], outs)}

    q_in = meet(q.astype(BF16), "z", 1)
    back = back_call(range(6, 12), dz_t)
    dz_t, q_in, back[3] = lax.optimization_barrier((dz_t, q_in, back[3]))

    up, down = shift(back[4], 1), shift(back[5], -1)
    q = q + q_in.astype(F32)
    q_in = meet(q.astype(BF16), "z", 2)
    back.update(back_call(range(12, 22), dz_t))
    dz_t, q_in, back[0] = lax.optimization_barrier((dz_t, q_in, back[0]))

    q = q + q_in.astype(F32)
    q_in = meet(q.astype(BF16), "z", 4)
    grads = call(
        grad_other_kernel,
        shape(NK, FEAT + VROWS, TOK),
        200_000_000,
        4 << 20,
        (place, index, x_all, dz_t),
    )
    up, down, q_in, grads = lax.optimization_barrier((up, down, q_in, grads))

    grads_in = meet(grads, "core", 1)
    up, down = shift(add(back[3], up), 1), shift(add(back[6], down), -1)
    q = q + q_in.astype(F32)
    q_in = meet(q.astype(BF16), "xh", 1)
    grads = call(
        grad_own_kernel,
        shape(NK, FEAT + VROWS + 2 * UROWS, TOK),
        200_000_000,
        6 << 20,
        (place, index, x_all, dz_t, grads_in),
    )
    up, down, q_in, grads = lax.optimization_barrier((up, down, q_in, grads))

    up, down = shift(add(back[2], up), 1), shift(add(back[7], down), -1)
    q_t = (q + q_in.astype(F32)).astype(BF16)
    grads = u_call(place, grads, x_all, q_t.reshape(SH, RS, TOK))
    up, down, _, q_t = lax.optimization_barrier((up, down, grads, q_t))

    up = shift(add(back[1], up), 1)
    other = add(back[0][1], up[1], down[1])
    total = add(back[0][0], up[0], down[0], meet(other, "xh", 1))
    x_grad_t = lax.ppermute(total, ALL, turn)
    grads_in = lax.all_to_all(grads, ("xl", "y"), 0, 0)
    q_turned = lax.ppermute(q_t, ALL, turn)

    grads_sum = jnp.sum(grads_in.astype(F32), axis=0)
    blocks_grad = (
        grads_sum[:FEAT]
        .astype(BF16)
        .reshape(NB // 2, BS, 2, BS)
        .transpose(0, 2, 1, 3)
        .reshape(sparse_blocks.shape)
    )
    v_grad = (
        grads_sum[FEAT : FEAT + VROWS]
        .reshape(WIDTH // TOK, RS, TOK)
        .transpose(1, 0, 2)
        .reshape(RS, WIDTH)
    )
    u_own = grads_sum[FEAT + VROWS : FEAT + VROWS + UROWS]
    u_other = grads_sum[FEAT + VROWS + UROWS :]
    u_grad = (
        (u_own + meet(u_other, "core", 1))
        .reshape(FEAT // TOK, RS, TOK)
        .transpose(0, 2, 1)
        .reshape(FEAT, RS)
    )
    x_grad_t, q_turned, blocks_grad, v_grad, u_grad = lax.optimization_barrier(
        (x_grad_t, q_turned, blocks_grad, v_grad, u_grad)
    )
    x_low = lax.dot_general(
        q_turned, u_factor, (((0,), (1,)), ((), ())), preferred_element_type=F32
    )
    input_grad = add(x_grad_t.T, x_low)
    return hidden, input_grad, blocks_grad, u_grad, v_grad


def solution(mesh):
    fine = Mesh(mesh.devices.reshape(8, 2, 2, 4, 2), ALL)
    in_specs = (
        P(ROW, COL),
        P(COL, ROW),
        P(COL, ROW, None, None),
        P(COL, ROW, None),
        P(COL, None),
        P(None, ROW),
    )
    out_specs = (
        P(COL, ROW),
        P(ROW, COL),
        P(COL, ROW, None, None),
        P(COL, ROW),
        P(COL, ROW),
    )
    return jax.shard_map(
        on_device, mesh=fine, in_specs=in_specs, out_specs=out_specs, check_vma=False
    )
```

```python
import functools

import jax
import jax.numpy as jnp
from jax import lax
from jax.experimental import pallas as pl
from jax.experimental.pallas import tpu as pltpu
from jax.sharding import Mesh, PartitionSpec as P

BS = 64
NB = 16
SH = 16
NZ = 8
NK = 8
FEAT = 512
WIDTH = 2048
TOK = 128
RANK = 256
RS = RANK // SH
ROWS = FEAT + RS
WROWS = FEAT + 16
VROWS = WIDTH // TOK * RS
UROWS = FEAT // TOK * RS
BCOLS = WIDTH // BS

ROW = ("z", "xh")
COL = ("xl", "y", "core")
ALL = ROW + COL

NN = (((1,), (0,)), ((), ()))
NT = (((1,), (1,)), ((), ()))
F32 = jnp.float32
BF16 = jnp.bfloat16


def dot(a, b, dims):
    return lax.dot_general(a, b, dims, preferred_element_type=F32)


def gelu_pair(z):
    half = 0.5 * (1.0 + lax.erf(z * 0.7071067811865476))
    slope = half + z * jnp.exp(-0.5 * z * z) * 0.3989422804014327
    return z * half, slope


def block_start(position):
    return pl.multiple_of(position * BS, BS)


def x_slot(place, s):
    return (((s >> 1) - place[0]) & (NZ - 1)) * 2 + ((s & 1) ^ place[1])


def x_shard(place, slot):
    return (((slot >> 1) + place[0]) & (NZ - 1)) * 2 + ((slot & 1) ^ place[1])


def first_kernel(x, u, x_t, p):
    x_t[...] = x[...].T
    p[...] = dot(u[...].T, x_t[...], NN).reshape(SH, RS, TOK)


def forward_kernel(place, index, *refs):
    x_parts = refs[:NZ]
    w, v, cot, hidden, dz_t, q_t, x, z_t, sems = refs[NZ:]
    copies = [
        pltpu.make_async_copy(x_parts[rel], x.at[2 * rel : 2 * rel + 2], sems.at[rel])
        for rel in range(NZ)
    ]
    for copy in copies:
        copy.start()
    z_t[...] = jnp.zeros_like(z_t)
    for copy in copies:
        copy.wait()

    def shard(slot, carry):
        s = x_shard(place, slot)
        sums = []
        for pair in range(NB // 2):
            both = w[s, pair * BS : (pair + 1) * BS, :].T
            for side in range(2):
                b = index[s, 2 * pair + side]
                x_block = x[slot, pl.ds(block_start(b // BCOLS), BS), :]
                sums.append((b % BCOLS, dot(both[side * BS : (side + 1) * BS], x_block, NN)))
        for where, value in sums:
            z_t[pl.ds(block_start(where), BS), :] += value
        return carry

    lax.fori_loop(0, SH, shard, 0)
    p = jnp.concatenate([x[x_slot(place, s), FEAT:, :] for s in range(SH)], axis=0).T
    for j in range(WIDTH // TOK):
        part = slice(j * TOK, (j + 1) * TOK)
        z = z_t[part, :].T + dot(p, v[:, part], NN)
        value, slope = gelu_pair(z)
        hidden[:, part] = value.astype(BF16)
        dz = cot[:, part].astype(F32) * slope
        dz_t[part, :] = dz.T.astype(BF16)
    q_t[...] = dot(v[...], dz_t[...], NN)


def back_kernel(slots, place, index, w, dz_t, *refs):
    outs = refs[: len(slots) // 2]
    total, done = refs[len(slots) // 2 :]

    def shard(i, carry):
        slot = (i + slots[0]) & (2 * NZ - 1)
        s = x_shard(place, slot)
        total[...] = jnp.zeros_like(total)
        sums = []
        for pair in range(NB // 2):
            both = w[s, pair * BS : (pair + 1) * BS, :]
            for side in range(2):
                b = index[s, 2 * pair + side]
                dz_block = dz_t[pl.ds(block_start(b % BCOLS), BS), :]
                sums.append((b // BCOLS, dot(both[:, side * BS : (side + 1) * BS], dz_block, NN)))
        for where, value in sums:
            total[pl.ds(block_start(where), BS), :] += value
        done[i] = total[...].astype(BF16)
        return carry

    lax.fori_loop(0, len(slots), shard, 0)
    for i in range(len(slots) // 2):
        outs[i][...] = done[2 * i : 2 * i + 2]


def grad_rows(place, index, x, dz_t, out, half, other):
    core = place[2] ^ half

    def plus(value, k, first):
        if other is not None:
            value += other[k, first : first + value.shape[0], :].astype(F32)
        return value.astype(BF16)

    def shard(k, carry):
        s = 2 * k + core
        slot = x_slot(place, s)
        for pair in range(NB // 2):
            halves = []
            for side in range(2):
                b = index[s, 2 * pair + side]
                x_block = x[slot, pl.ds(block_start(b // BCOLS), BS), :]
                dz_block = dz_t[pl.ds(block_start(b % BCOLS), BS), :]
                halves.append(dot(x_block, dz_block, NT))
            both = jnp.concatenate(halves, axis=1)
            out[k, pair * BS : (pair + 1) * BS, :] = plus(both, k, pair * BS)
        return carry

    lax.fori_loop(0, NK, shard, 0)
    p = jnp.concatenate([x[x_slot(place, 2 * k + core), FEAT:, :] for k in range(NK)], axis=0)
    for j in range(WIDTH // TOK):
        part = dot(p, dz_t[j * TOK : (j + 1) * TOK, :], NT)
        first = FEAT + j * RS
        for k in range(NK):
            out[k, first : first + RS, :] = plus(part[k * RS : (k + 1) * RS], k, first)


def grad_other_kernel(place, index, x, dz_t, out):
    grad_rows(place, index, x, dz_t, out, 1, None)


def grad_own_kernel(place, index, x, dz_t, other, out):
    grad_rows(place, index, x, dz_t, out, 0, other)


def u_kernel(place, grads, x, q_t, out, rows, sem):
    q = q_t[place[3]]

    def shard(k, carry):
        for half in range(2):
            slot = x_slot(place, 2 * k + (place[2] ^ half))
            u = dot(q, x[slot, :FEAT, :], NT).astype(BF16)
            for j in range(FEAT // TOK):
                first = half * UROWS + j * RS
                rows[k, first : first + RS, :] = u[:, j * TOK : (j + 1) * TOK]
        return carry

    lax.fori_loop(0, NK, shard, 0)
    copy = pltpu.make_async_copy(rows, out.at[:, FEAT + VROWS :, :], sem)
    copy.start()
    copy.wait()


def u_call(place, grads, x, q_t):
    vmem = pl.BlockSpec(memory_space=pltpu.VMEM)
    anywhere = pl.BlockSpec(memory_space=pl.ANY)
    return pl.pallas_call(
        u_kernel,
        out_shape=jax.ShapeDtypeStruct(grads.shape, BF16),
        in_specs=[pl.BlockSpec(memory_space=pltpu.SMEM), anywhere, vmem, vmem],
        out_specs=anywhere,
        scratch_shapes=[pltpu.VMEM((NK, 2 * UROWS, TOK), BF16), pltpu.SemaphoreType.DMA],
        input_output_aliases={1: 0},
        compiler_params=pltpu.CompilerParams(vmem_limit_bytes=10 << 20),
        cost_estimate=pl.CostEstimate(
            flops=70_000_000, bytes_accessed=3 << 20, transcendentals=0
        ),
    )(place, grads, x, q_t)


def call(kernel, out_shape, flops, bytes_accessed, operands, scratch=(), free=0, scalars=2):
    vmem = pl.BlockSpec(memory_space=pltpu.VMEM)
    smem = pl.BlockSpec(memory_space=pltpu.SMEM)
    anywhere = pl.BlockSpec(memory_space=pl.ANY)
    many = isinstance(out_shape, tuple)
    return pl.pallas_call(
        kernel,
        out_shape=out_shape,
        in_specs=[smem] * scalars + [anywhere] * free + [vmem] * (len(operands) - scalars - free),
        out_specs=(vmem,) * len(out_shape) if many else vmem,
        scratch_shapes=list(scratch),
        compiler_params=pltpu.CompilerParams(vmem_limit_bytes=10 << 20),
        cost_estimate=pl.CostEstimate(
            flops=flops, bytes_accessed=bytes_accessed, transcendentals=0
        ),
    )(*operands)


def shape(*dims, kind=BF16):
    return jax.ShapeDtypeStruct(dims, kind)


def add(*terms):
    return sum(t.astype(F32) for t in terms).astype(BF16)


def shift(x, by):
    return lax.ppermute(x, "z", [(i, (i + by) % NZ) for i in range(NZ)])


def meet(x, axis, flip):
    count = {"z": 8, "xh": 2, "xl": 2, "y": 4, "core": 2}[axis]
    return lax.ppermute(x, axis, [(i, i ^ flip) for i in range(count)])


def on_device(inputs, cotangent, sparse_blocks, block_index, u_factor, v_factor):
    turn = [(r * SH + c, c * SH + r) for r in range(SH) for c in range(SH)]
    turn_pair = [(r * SH + c, (c ^ 1) * SH + r) for r in range(SH) for c in range(SH)]
    place = jnp.stack(
        [lax.axis_index("z"), lax.axis_index("xh"), lax.axis_index("core"), lax.axis_index(ROW)]
    ).astype(jnp.int32)

    w_pairs = sparse_blocks.reshape(NB // 2, 2, BS, BS).transpose(0, 2, 1, 3).reshape(FEAT, 2 * BS)
    index_row = jnp.zeros((16, TOK), BF16).at[0, :NB].set(block_index.reshape(NB).astype(BF16))
    w_mine = jnp.concatenate([w_pairs, index_row])
    w_mine, inputs = lax.optimization_barrier((w_mine, inputs))
    w_all = lax.all_gather(w_mine, COL, axis=0)

    mine, p = call(
        first_kernel,
        (shape(FEAT, TOK), shape(SH, RS, TOK, kind=F32)),
        40_000_000,
        1 << 19,
        (inputs, u_factor),
        scalars=0,
    )
    turned = lax.ppermute(mine, ALL, turn)
    p_in = lax.all_to_all(p, COL, 0, 0)
    turned, p_in = lax.optimization_barrier((turned, p_in))
    p = jnp.sum(p_in, axis=0).astype(BF16)
    parts = [
        turned,
        lax.ppermute(p, ALL, turn),
        meet(turned, "xh", 1),
        lax.ppermute(p, ALL, turn_pair),
    ]
    held = {0: jnp.concatenate(parts).reshape(2, ROWS, TOK)}
    for step in (1, 2, 3):
        held[-step], held[step] = shift(held[1 - step], 1), shift(held[step - 1], -1)
        if step == 2:
            w_all, held[-2], held[2] = lax.optimization_barrier((w_all, held[-2], held[2]))
    held[4] = shift(held[-3], 1)
    x_parts = [held[rel if rel <= 4 else rel - NZ] for rel in range(NZ)]
    index = w_all[:, FEAT, :NB].astype(jnp.int32)

    hidden, dz_t, q, x_all = call(
        forward_kernel,
        (
            shape(TOK, WIDTH),
            shape(WIDTH, TOK),
            shape(RANK, TOK, kind=F32),
            shape(SH, ROWS, TOK),
        ),
        800_000_000,
        10 << 20,
        (place, index, *x_parts, w_all, v_factor, cotangent),
        [pltpu.VMEM((WIDTH, TOK), F32), pltpu.SemaphoreType.DMA((NZ,))],
        free=NZ,
    )

    def back_call(slots, dz_back):
        outs = call(
            functools.partial(back_kernel, slots),
            (shape(2, FEAT, TOK),) * (len(slots) // 2),
            20_000_000 * len(slots),
            len(slots) << 19,
            (place, index, w_all, dz_back),
            [pltpu.VMEM((FEAT, TOK), F32), pltpu.VMEM((len(slots), FEAT, TOK), BF16)],
        )
        return {slot // 2 % NZ: part for slot, part in zip(slots[::2], outs)}

    q_in = meet(q.astype(BF16), "z", 1)
    back = back_call(range(6, 12), dz_t)
    dz_t, q_in, back[3] = lax.optimization_barrier((dz_t, q_in, back[3]))

    up, down = shift(back[4], 1), shift(back[5], -1)
    q = q + q_in.astype(F32)
    q_in = meet(q.astype(BF16), "z", 2)
    back.update(back_call(range(12, 22), dz_t))
    dz_t, q_in, back[0] = lax.optimization_barrier((dz_t, q_in, back[0]))

    q = q + q_in.astype(F32)
    q_in = meet(q.astype(BF16), "z", 4)
    grads = call(
        grad_other_kernel,
        shape(NK, FEAT + VROWS, TOK),
        200_000_000,
        4 << 20,
        (place, index, x_all, dz_t),
    )
    up, down, q_in, grads = lax.optimization_barrier((up, down, q_in, grads))

    grads_in = meet(grads, "core", 1)
    up, down = shift(add(back[3], up), 1), shift(add(back[6], down), -1)
    q = q + q_in.astype(F32)
    q_in = meet(q.astype(BF16), "xh", 1)
    grads = call(
        grad_own_kernel,
        shape(NK, FEAT + VROWS + 2 * UROWS, TOK),
        200_000_000,
        6 << 20,
        (place, index, x_all, dz_t, grads_in),
    )
    up, down, grads = lax.optimization_barrier((up, down, grads))

    up, down = shift(add(back[2], up), 1), shift(add(back[7], down), -1)
    q_t = (q + q_in.astype(F32)).astype(BF16)
    grads = u_call(place, grads, x_all, q_t.reshape(SH, RS, TOK))
    up, down, _, q_t = lax.optimization_barrier((up, down, grads, q_t))

    up = shift(add(back[1], up), 1)
    other = add(back[0][1], up[1], down[1])
    total = add(back[0][0], up[0], down[0], meet(other, "xh", 1))
    x_grad_t = lax.ppermute(total, ALL, turn)
    grads_in = lax.all_to_all(grads, ("xl", "y"), 0, 0)
    q_turned = lax.ppermute(q_t, ALL, turn)

    grads_sum = jnp.sum(grads_in.astype(F32), axis=0)
    blocks_grad = (
        grads_sum[:FEAT]
        .astype(BF16)
        .reshape(NB // 2, BS, 2, BS)
        .transpose(0, 2, 1, 3)
        .reshape(sparse_blocks.shape)
    )
    v_grad = (
        grads_sum[FEAT : FEAT + VROWS]
        .reshape(WIDTH // TOK, RS, TOK)
        .transpose(1, 0, 2)
        .reshape(RS, WIDTH)
    )
    u_own = grads_sum[FEAT + VROWS : FEAT + VROWS + UROWS]
    u_other = grads_sum[FEAT + VROWS + UROWS :]
    u_grad = (
        (u_own + meet(u_other, "core", 1))
        .reshape(FEAT // TOK, RS, TOK)
        .transpose(0, 2, 1)
        .reshape(FEAT, RS)
    )
    x_grad_t, q_turned, blocks_grad, v_grad, u_grad = lax.optimization_barrier(
        (x_grad_t, q_turned, blocks_grad, v_grad, u_grad)
    )
    x_low = lax.dot_general(
        q_turned, u_factor, (((0,), (1,)), ((), ())), preferred_element_type=F32
    )
    input_grad = add(x_grad_t.T, x_low)
    return hidden, input_grad, blocks_grad, u_grad, v_grad


def solution(mesh):
    fine = Mesh(mesh.devices.reshape(8, 2, 2, 4, 2), ALL)
    in_specs = (
        P(ROW, COL),
        P(COL, ROW),
        P(COL, ROW, None, None),
        P(COL, ROW, None),
        P(COL, None),
        P(None, ROW),
    )
    out_specs = (
        P(COL, ROW),
        P(ROW, COL),
        P(COL, ROW, None, None),
        P(COL, ROW),
        P(COL, ROW),
    )
    return jax.shard_map(
        on_device, mesh=fine, in_specs=in_specs, out_specs=out_specs, check_vma=False
    )
```
